512 devices in a mesh: tm: 32 (over z, core), space: 16 (over x, y).
Axes of the slice: x: 4, y: 4, z: 16, core: 2. Of those that a mesh axis runs over, the one named last changes fastest.
Arguments:
- queries: bfloat16 [32, 4096, 2048], P('tm', 'space'), may hold values from -30 to 30
- keys: bfloat16 [32, 4096, 2048], P('tm', 'space'), may hold values from -30 to 30
- values: bfloat16 [32, 4096, 2048], P('tm', 'space'), may hold values from -6 to 6
- groups: int32 [32, 4096], P('tm', 'space'), may hold values from 0 to 511, as said below
Outputs:
- attended: bfloat16 [32, 4096, 2048], P('tm', 'space')
The draws below stay inside these ranges and needn't reach their ends.
Inputs may be any that keep to these rules, and one draw needn't show every extreme that they name: `groups`: each of the 512 group numbers is held by exactly 256 tokens.
All inputs are finite; a program needn't handle non-finite values.
Results may differ from the reference program's by a relative error of at most 0.012.
Values may be sent and summed in bfloat16 or wider, within the bound.
No kernel may reach another device: no remote copies, remote signals or barrier semaphores. Data moves between devices by JAX's collectives and lax.ppermute only.
A program may use at most 128 MiB of HBM per device.

```python
import math
import jax
import jax.numpy as jnp
from jax import lax

HEADS = 16
HEAD_DIM = 128
LANDMARKS = 512
ITERS = 3
FRAMES = 32
POSITIONS = 4096
GROUP = 256


def member_ids(key):
    order = jax.random.permutation(jax.random.fold_in(key, 5), FRAMES * POSITIONS)
    return (order // GROUP).astype(jnp.int32).reshape(FRAMES, POSITIONS)


def shared_parts(key):
    width = HEADS * HEAD_DIM
    query_part = jax.random.normal(jax.random.fold_in(key, 11), (LANDMARKS, width), jnp.float32)
    other_part = jax.random.normal(jax.random.fold_in(key, 12), (LANDMARKS, width), jnp.float32)
    direction = jax.random.normal(jax.random.fold_in(key, 13), (width,), jnp.float32)
    return (query_part, 0.53 * query_part + 0.85 * other_part, direction)


def noisy_tokens(key, table, ids, direction, reach):
    noise = 0.5 * jax.random.normal(key, (FRAMES, POSITIONS, HEADS * HEAD_DIM), jnp.float32)
    result = jnp.take(table, ids, axis=0) + noise
    strength = jax.random.uniform(jax.random.fold_in(key, 7), (FRAMES, POSITIONS, 1), jnp.float32, 0.0, reach)
    result = result + strength * direction
    return jnp.clip(result, -30.0, 30.0).astype(jnp.bfloat16)


def draw_groups(key, part):
    return member_ids(key)


def draw_queries(key, part):
    ids = member_ids(key)
    query_part, key_part, direction = shared_parts(key)
    key = jax.random.fold_in(key, 2)
    return noisy_tokens(key, query_part, ids, direction, 0.0)


def draw_keys(key, part):
    ids = member_ids(key)
    query_part, key_part, direction = shared_parts(key)
    key = jax.random.fold_in(key, 3)
    return noisy_tokens(key, key_part, ids, direction, 0.0)


def shard_levels(stream_key, shape, pieces, smallest, high):
    def one(position, blocks):
        steps = jax.random.uniform(jax.random.fold_in(jax.random.fold_in(stream_key, 6), position), (blocks,), jnp.float32, smallest / len(pieces), high / len(pieces))
        return jnp.repeat(jnp.exp(steps), shape[position] // blocks).reshape((-1,) + (1,) * (len(shape) - position - 1))

    gain = one(*pieces[0])
    for cut in pieces[1:]:
        gain = gain * one(*cut)
    return gain


def scatter_about(key, shape, spread, most, cuts=(), kind=jnp.bfloat16):
    drawn = jax.random.normal(key, shape, jnp.float32) * spread
    if len(cuts) > 0:
        drawn = shard_levels(key, shape, cuts, -0.22, 0.18) * drawn
    return jnp.clip(drawn, min=-most, max=most).astype(kind)


def setup_inputs(seed: int = 0) -> dict:
    key_list = jax.random.split(jax.random.key(seed), 5)
    return {
        "queries": draw_queries(jax.random.fold_in(key_list[4], 71), 0),
        "keys": draw_keys(jax.random.fold_in(key_list[4], 71), 0),
        "values": scatter_about(key_list[2], (FRAMES, POSITIONS, HEADS * HEAD_DIM), 1.0, 6.0, ((0, 32), (1, 16))),
        "groups": draw_groups(jax.random.fold_in(key_list[4], 71), 0),
    }


def softmax_rows(logits):
    ceiling = lax.optimization_barrier(jnp.max(logits, axis=-1, keepdims=True))
    expo = jnp.exp(logits - ceiling)
    return expo / lax.optimization_barrier(jnp.sum(expo, axis=-1, keepdims=True))

def pseudo_inverse(kernel):
    highest = lax.Precision.HIGHEST
    column_top = jnp.max(lax.optimization_barrier(jnp.sum(kernel, axis=0)))
    iterate = kernel.T / column_top
    for step in range(ITERS):
        product = jnp.dot(kernel, iterate, precision=highest)
        first = jnp.dot(iterate, product, precision=highest)
        second = jnp.dot(first, product, precision=highest)
        third = jnp.dot(second, product, precision=highest)
        iterate = 0.25 * (13.0 * iterate - 15.0 * first + 7.0 * second - third)
    return iterate

def reference(queries, keys, values, groups):
    frames, positions, width = queries.shape
    scale = 1.0 / math.sqrt(HEAD_DIM)
    q_four = queries.reshape(frames, positions, HEADS, HEAD_DIM)
    k_four = keys.reshape(frames, positions, HEADS, HEAD_DIM)
    v_four = values.reshape(frames, positions, HEADS, HEAD_DIM)
    member = groups.reshape(-1)
    landmark_ids = jnp.arange(LANDMARKS, dtype=jnp.int32)

    def one_head(index):
        q_head = lax.dynamic_index_in_dim(q_four, index, 2, keepdims=False)
        k_head = lax.dynamic_index_in_dim(k_four, index, 2, keepdims=False)
        v_head = lax.dynamic_index_in_dim(v_four, index, 2, keepdims=False)
        logits = jnp.einsum('fse,gse->sfg', q_head.astype(jnp.float32), k_head.astype(jnp.float32)) * scale
        weights = softmax_rows(logits).astype(jnp.bfloat16)
        temporal = jnp.einsum('sfg,gse->fse', weights.astype(jnp.float32), v_head.astype(jnp.float32)).astype(jnp.bfloat16)
        q_flat = q_head.reshape(-1, HEAD_DIM)
        k_flat = k_head.reshape(-1, HEAD_DIM)
        onehot = (member[None, :] == landmark_ids[:, None]).astype(jnp.bfloat16)
        q_land = (jnp.dot(onehot, q_flat, preferred_element_type=jnp.float32) / GROUP).astype(jnp.bfloat16)
        k_land = (jnp.dot(onehot, k_flat, preferred_element_type=jnp.float32) / GROUP).astype(jnp.bfloat16)
        kernel = softmax_rows(jnp.dot(q_land, k_land.T, preferred_element_type=jnp.float32) * scale)
        inverse = pseudo_inverse(kernel)
        land_logits = (jnp.dot(q_land, k_flat.T, preferred_element_type=jnp.float32) * scale).reshape(LANDMARKS, frames, positions)
        frame_top = lax.optimization_barrier(jnp.max(land_logits, axis=-1))
        frame_weights = jnp.exp(land_logits - frame_top[..., None])
        frame_total = lax.optimization_barrier(jnp.sum(frame_weights, axis=-1))
        frame_sum = jnp.einsum('mfs,fse->mfe', frame_weights.astype(jnp.bfloat16).astype(jnp.float32), temporal.astype(jnp.float32))
        top = lax.optimization_barrier(jnp.max(frame_top, axis=-1))
        factor = jnp.exp(frame_top - top[:, None])
        total = lax.optimization_barrier(jnp.sum(frame_total * factor, axis=-1))
        weighted = lax.optimization_barrier(jnp.sum(frame_sum * factor[..., None], axis=1))
        summary = weighted / total[:, None]
        mixed = jnp.dot(inverse, summary, precision=lax.Precision.HIGHEST).astype(jnp.bfloat16)
        token_logits = jnp.dot(q_flat, k_land.T, preferred_element_type=jnp.float32) * scale
        attend = softmax_rows(token_logits).astype(jnp.bfloat16)
        global_part = jnp.dot(attend, mixed, preferred_element_type=jnp.float32)
        return (temporal.reshape(-1, HEAD_DIM).astype(jnp.float32) + global_part).astype(jnp.bfloat16)
    outputs = lax.map(one_head, jnp.arange(HEADS, dtype=jnp.int32))
    return jnp.transpose(outputs, (1, 0, 2)).reshape(frames, positions, HEADS * HEAD_DIM)
```

```python
import math

import jax
import jax.numpy as jnp
from jax import lax
from jax.sharding import PartitionSpec as P

HEAD_DIM = 128
LANDMARKS = 512
ITERS = 3
BOTH = ("tm", "space")


def softmax_rows(logits):
    ceiling = jnp.max(logits, axis=-1, keepdims=True)
    expo = jnp.exp(logits - ceiling)
    return expo / jnp.sum(expo, axis=-1, keepdims=True)


def product(left, right):
    return jnp.dot(left, right, precision=lax.Precision.HIGHEST)


def swap(x, axes):
    return lax.all_to_all(x, axes, split_axis=0, concat_axis=0, tiled=True)


def share(x, axis):
    size = lax.axis_size(axis)
    return swap(jnp.broadcast_to(x[None], (size,) + x.shape), axis)


def total_over(x):
    size = lax.axis_size("tm")
    rows, width = x.shape
    parts = swap(x.astype(jnp.bfloat16).reshape(size, rows // size, width), "tm")
    return jnp.sum(parts.astype(jnp.float32), axis=0)


def local(queries, keys, values, groups):
    frames, count, width = queries.shape
    heads = width // HEAD_DIM
    scale = 1.0 / math.sqrt(HEAD_DIM)
    tm, space = lax.axis_size("tm"), lax.axis_size("space")
    few = count // tm

    def tiles(x):
        x = x.reshape(tm, few, heads, HEAD_DIM)
        return jnp.swapaxes(x, 1, 2).reshape(tm * heads, few, HEAD_DIM)

    qk = jnp.stack([tiles(queries), tiles(keys)], axis=1)
    qk = swap(qk, BOTH)
    v = swap(tiles(values), BOTH)
    member = swap(groups.reshape(tm, few), "tm")
    member = lax.all_gather(member, "space")
    member = jnp.swapaxes(member, 0, 1).reshape(-1)

    tokens = tm * space * few
    q = qk[:, 0].reshape(tokens, HEAD_DIM)
    k = qk[:, 1].reshape(tokens, HEAD_DIM)
    v = v.reshape(tokens, HEAD_DIM)

    landmark_ids = jnp.arange(LANDMARKS, dtype=jnp.int32)
    onehot = (member[None, :] == landmark_ids[:, None]).astype(jnp.bfloat16)
    q_part = jnp.dot(onehot, q, preferred_element_type=jnp.float32)
    k_part = jnp.dot(onehot, k, preferred_element_type=jnp.float32)
    block = LANDMARKS // tm
    both = jnp.concatenate(
        [q_part.reshape(tm, block, HEAD_DIM), k_part.reshape(tm, block, HEAD_DIM)], axis=1
    )
    sums = total_over(both.reshape(2 * LANDMARKS, HEAD_DIM))
    members_each = tm * tokens // LANDMARKS
    lands = share((sums / members_each).astype(jnp.bfloat16), "tm")
    q_land = lands[:, :block].reshape(LANDMARKS, HEAD_DIM)
    k_land = lands[:, block:].reshape(LANDMARKS, HEAD_DIM)

    def split(x):
        x = x.reshape(tm, space, few, HEAD_DIM)
        return jnp.swapaxes(x, 0, 1).reshape(space, tm * few, HEAD_DIM)

    qs, ks, vs = split(q), split(k), split(v)
    logits = jnp.einsum("sae,sbe->sab", qs, ks, preferred_element_type=jnp.float32) * scale
    index = jnp.arange(tm * few, dtype=jnp.int32) % few
    logits = jnp.where(index[:, None] == index[None, :], logits, -jnp.inf)
    weights = softmax_rows(logits).astype(jnp.bfloat16)
    temporal = jnp.einsum("sab,sbe->sae", weights, vs, preferred_element_type=jnp.float32)
    temporal = temporal.astype(jnp.bfloat16).reshape(space, tm, few, HEAD_DIM)
    temporal = jnp.swapaxes(temporal, 0, 1).reshape(tokens, HEAD_DIM)

    kernel = softmax_rows(
        jnp.einsum("me,ne->mn", q_land, k_land, preferred_element_type=jnp.float32) * scale
    )
    column_top = jnp.max(jnp.sum(kernel, axis=0))
    iterate = kernel.T / column_top
    for step in range(ITERS):
        gain = product(kernel, iterate)
        first = product(iterate, gain)
        second = product(first, gain)
        third = product(second, gain)
        iterate = 0.25 * (13.0 * iterate - 15.0 * first + 7.0 * second - third)

    land_logits = jnp.einsum("me,se->ms", q_land, k, preferred_element_type=jnp.float32) * scale
    own_top = jnp.max(land_logits, axis=-1)
    own_weights = jnp.exp(land_logits - own_top[:, None])
    own_total = jnp.sum(own_weights, axis=-1)
    pair = share(jnp.stack([own_top, own_total]).reshape(-1, 128), "tm")
    pair = pair.reshape(tm, 2, LANDMARKS)
    top = jnp.max(pair[:, 0], axis=0)
    total = jnp.sum(pair[:, 1] * jnp.exp(pair[:, 0] - top), axis=0)
    own_sum = jnp.dot(own_weights.astype(jnp.bfloat16), temporal, preferred_element_type=jnp.float32)
    share_of = jnp.exp(own_top - top) / total
    summary = total_over(own_sum * share_of[:, None])
    summary = share(summary.astype(jnp.bfloat16), "tm").reshape(LANDMARKS, HEAD_DIM)
    mixed = product(iterate, summary.astype(jnp.float32)).astype(jnp.bfloat16)

    token_logits = jnp.einsum("se,me->sm", q, k_land, preferred_element_type=jnp.float32) * scale
    attend = softmax_rows(token_logits).astype(jnp.bfloat16)
    global_part = jnp.dot(attend, mixed, preferred_element_type=jnp.float32)
    combined = (temporal.astype(jnp.float32) + global_part).astype(jnp.bfloat16)
    back = swap(combined.reshape(tm * space, few, HEAD_DIM), BOTH)
    back = jnp.swapaxes(back.reshape(tm, heads, few, HEAD_DIM), 1, 2)
    return back.reshape(frames, count, width)


def solution(mesh):
    return jax.shard_map(
        local,
        mesh=mesh,
        in_specs=(
            P("tm", "space", None),
            P("tm", "space", None),
            P("tm", "space", None),
            P("tm", "space"),
        ),
        out_specs=P("tm", "space", None),
        check_vma=False,
    )
```

```python
import math

import jax
import jax.numpy as jnp
from jax import lax
from jax.experimental import pallas as pl
from jax.experimental.pallas import tpu as pltpu
from jax.sharding import PartitionSpec as P

HEAD_DIM = 128
LANDMARKS = 512
ITERS = 3
ACROSS = ("z", "core")
PLANE = ("core", "space")
SCALE = 1.0 / math.sqrt(HEAD_DIM)
F32 = jnp.float32
BF16 = jnp.bfloat16


def softmax_rows(logits):
    ceiling = jnp.max(logits, axis=-1, keepdims=True)
    expo = jnp.exp(logits - ceiling)
    return expo / jnp.sum(expo, axis=-1, keepdims=True)


def halves(x):
    high = x.astype(BF16)
    return high, (x - high.astype(F32)).astype(BF16)


def triple(left, right):
    lh, ll = left
    rh, rl = right
    out = jnp.dot(lh, rh, preferred_element_type=F32)
    out += jnp.dot(lh, rl, preferred_element_type=F32)
    return out + jnp.dot(ll, rh, preferred_element_type=F32)


def inverse_body(q_ref, k_ref, out_ref, kh_ref, kl_ref):
    dims = (((1,), (1,)), ((), ()))
    q, k = q_ref[...], k_ref[...]
    logits = lax.dot_general(q, k, dims, preferred_element_type=F32) * SCALE
    kernel = softmax_rows(logits)
    column_top = jnp.max(jnp.sum(kernel, axis=0, keepdims=True))
    kh_ref[...], kl_ref[...] = halves(kernel)
    logits = lax.dot_general(k, q, dims, preferred_element_type=F32) * SCALE
    expo = jnp.exp(logits - jnp.max(logits, axis=0, keepdims=True))
    out_ref[...] = expo / (jnp.sum(expo, axis=0, keepdims=True) * column_top)

    def step(_, carry):
        iterate = out_ref[...]
        z = halves(iterate)
        y = halves(triple((kh_ref[...], kl_ref[...]), z))
        first = triple(z, y)
        second = triple(halves(first), y)
        third = triple(halves(second), y)
        out_ref[...] = 0.25 * (13.0 * iterate - 15.0 * first + 7.0 * second - third)
        return carry

    lax.fori_loop(0, ITERS, step, 0)


def pseudo_inverse(q_land, k_land):
    whole = pl.BlockSpec(memory_space=pltpu.VMEM)
    return pl.pallas_call(
        inverse_body,
        out_shape=jax.ShapeDtypeStruct((LANDMARKS, LANDMARKS), F32),
        in_specs=[whole, whole],
        out_specs=whole,
        scratch_shapes=[pltpu.VMEM((LANDMARKS, LANDMARKS), BF16)] * 2,
        compiler_params=pltpu.CompilerParams(vmem_limit_bytes=32 * 2**20),
        cost_estimate=pl.CostEstimate(
            flops=12 * 3 * 2 * LANDMARKS**3, bytes_accessed=2 * 2**20, transcendentals=0
        ),
    )(q_land, k_land)


def pack_body(q_ref, k_ref, v_ref, id_ref, out_ref):
    sides, part = id_ref.shape
    quad = out_ref.shape[0] // sides
    row = lax.broadcasted_iota(jnp.int32, (16, part), 0)
    for side in range(sides):
        ids = id_ref[side : side + 1, :]
        coarse = lax.shift_right_logical(ids, 8)
        fine = ids - coarse * 256
        tile = jnp.where(row == 0, coarse, jnp.where(row == 1, fine, 0))
        tile = tile.astype(F32).astype(BF16)
        rows = slice(side * part, (side + 1) * part)
        for head in range(quad):
            lanes = slice(head * HEAD_DIM, (head + 1) * HEAD_DIM)
            chunk = head * sides + side
            out_ref[chunk, :part, :] = q_ref[rows, lanes]
            out_ref[chunk, part : 2 * part, :] = k_ref[rows, lanes]
            out_ref[chunk, 2 * part : 3 * part, :] = v_ref[rows, lanes]
            out_ref[chunk, 3 * part : 3 * part + 16, :] = tile


def pack(queries, keys, values, groups, sides):
    count, width = queries.shape
    part = count // sides
    quad = 4
    columns = quad * HEAD_DIM
    cut = pl.BlockSpec((count, columns), lambda i: (0, i))
    rows = 3 * part + 16
    chunks = width // HEAD_DIM * sides
    return pl.pallas_call(
        pack_body,
        grid=(width // columns,),
        out_shape=jax.ShapeDtypeStruct((chunks, rows, HEAD_DIM), BF16),
        in_specs=[cut, cut, cut, pl.BlockSpec((sides, part), lambda i: (0, 0))],
        out_specs=pl.BlockSpec((quad * sides, rows, HEAD_DIM), lambda i: (i, 0, 0)),
        compiler_params=pltpu.CompilerParams(vmem_limit_bytes=24 * 2**20),
    )(queries, keys, values, groups.reshape(sides, part))


def unpack_body(in_ref, out_ref):
    chunks, part, _ = in_ref.shape
    sides = out_ref.shape[0] // part
    for chunk in range(chunks):
        head, side = chunk // sides, chunk % sides
        rows = slice(side * part, (side + 1) * part)
        out_ref[rows, head * HEAD_DIM : (head + 1) * HEAD_DIM] = in_ref[chunk]


def unpack(x, sides):
    chunks, part, _ = x.shape
    quad = 4
    return pl.pallas_call(
        unpack_body,
        grid=(chunks // sides // quad,),
        out_shape=jax.ShapeDtypeStruct((sides * part, chunks // sides * HEAD_DIM), BF16),
        in_specs=[pl.BlockSpec((quad * sides, part, HEAD_DIM), lambda i: (i, 0, 0))],
        out_specs=pl.BlockSpec((sides * part, quad * HEAD_DIM), lambda i: (0, i)),
        compiler_params=pltpu.CompilerParams(vmem_limit_bytes=24 * 2**20),
    )(x)


def swap(x, axes):
    return lax.all_to_all(x, axes, split_axis=0, concat_axis=0, tiled=True)


def share(x, axes):
    size = lax.axis_size(axes)
    return swap(jnp.broadcast_to(x[None], (size,) + x.shape), axes)


def local(queries, keys, values, groups):
    frames, count, width = queries.shape
    heads = width // HEAD_DIM
    sides = lax.axis_size("core")
    steps = heads * sides
    part = count // sides
    tokens = steps * part
    plane = lax.axis_size(PLANE)
    block = LANDMARKS // plane

    packed = pack(queries[0], keys[0], values[0], groups, sides)
    got = swap(packed, ACROSS)
    q = got[:, :part].reshape(tokens, HEAD_DIM)
    k = got[:, part : 2 * part].reshape(tokens, HEAD_DIM)
    v = got[:, 2 * part : 3 * part].reshape(tokens, HEAD_DIM)
    ids = got[:, 3 * part : 3 * part + 2].astype(F32)
    member = (ids[:, 0] * 256.0 + ids[:, 1]).astype(jnp.int32).reshape(tokens)

    landmark_ids = jnp.arange(LANDMARKS, dtype=jnp.int32)
    onehot = (member[None, :] == landmark_ids[:, None]).astype(BF16)
    q_part = jnp.dot(onehot, q, preferred_element_type=F32).astype(BF16)
    k_part = jnp.dot(onehot, k, preferred_element_type=F32).astype(BF16)
    members_each = plane * tokens // LANDMARKS
    both = jnp.concatenate(
        [q_part.reshape(plane, block, HEAD_DIM), k_part.reshape(plane, block, HEAD_DIM)], axis=1
    )
    sums = jnp.sum(swap(both, PLANE).astype(F32), axis=0)
    lands = share((sums / members_each).astype(BF16), PLANE)
    q_land = lands[:, :block].reshape(LANDMARKS, HEAD_DIM)
    k_land = lands[:, block:].reshape(LANDMARKS, HEAD_DIM)

    few = 8

    def split(x):
        x = x.reshape(steps, part // few, few, HEAD_DIM)
        return jnp.swapaxes(x, 0, 1).reshape(part // few, steps * few, HEAD_DIM)

    logits = jnp.einsum("sae,sbe->sab", split(q), split(k), preferred_element_type=F32) * SCALE
    index = jnp.arange(steps * few, dtype=jnp.int32) % few
    logits = jnp.where(index[:, None] == index[None, :], logits, -jnp.inf)
    weights = softmax_rows(logits).astype(BF16)
    temporal = jnp.einsum("sab,sbe->sae", weights, split(v), preferred_element_type=F32)
    temporal = temporal.astype(BF16).reshape(part // few, steps, few, HEAD_DIM)
    temporal = jnp.swapaxes(temporal, 0, 1).reshape(tokens, HEAD_DIM)

    land_logits = jnp.einsum("me,se->ms", q_land, k, preferred_element_type=F32) * SCALE
    own_top = jnp.max(land_logits, axis=-1, keepdims=True).astype(BF16)
    own_weights = jnp.exp(land_logits - own_top.astype(F32))
    own_total = jnp.sum(own_weights, axis=-1, keepdims=True)
    own_sum = jnp.dot(own_weights.astype(BF16), temporal, preferred_element_type=F32)
    high, low = halves(own_total)
    extra = jnp.pad(
        jnp.concatenate([own_top, high, low], axis=1), ((0, 0), (0, HEAD_DIM - 3))
    )
    own = jnp.concatenate([own_sum.astype(BF16), extra], axis=1)
    parts = swap(own.reshape(plane, block, 2 * HEAD_DIM), PLANE).astype(F32)
    tops = parts[:, :, HEAD_DIM : HEAD_DIM + 1]
    totals = parts[:, :, HEAD_DIM + 1 : HEAD_DIM + 2] + parts[:, :, HEAD_DIM + 2 : HEAD_DIM + 3]
    factor = jnp.exp(tops - jnp.max(tops, axis=0))
    weighted = jnp.sum(parts[:, :, :HEAD_DIM] * factor, axis=0)
    summary = (weighted / jnp.sum(totals * factor, axis=0)).astype(BF16)
    summary = share(summary, PLANE).reshape(LANDMARKS, HEAD_DIM).astype(F32)

    inverse = pseudo_inverse(q_land, k_land)
    token_logits = jnp.einsum("se,me->sm", q, k_land, preferred_element_type=F32) * SCALE
    attend = lax.optimization_barrier(softmax_rows(token_logits).astype(BF16))
    mixed = jnp.dot(inverse, summary, precision=lax.Precision.HIGHEST).astype(BF16)
    global_part = jnp.dot(attend, mixed, preferred_element_type=F32)
    combined = (temporal.astype(F32) + global_part).astype(BF16)
    back = swap(combined.reshape(steps, part, HEAD_DIM), ACROSS)
    return unpack(back, sides)[None]


def solution(mesh):
    tm, space = mesh.devices.shape
    fine = jax.sharding.Mesh(mesh.devices.reshape(tm // 2, 2, space), ("z", "core", "space"))
    block = P(("z", "core"), "space", None)
    return jax.shard_map(
        local,
        mesh=fine,
        in_specs=(block, block, block, P(("z", "core"), "space")),
        out_specs=block,
        check_vma=False,
    )
```

```python
import math

import jax
import jax.numpy as jnp
from jax import lax
from jax.experimental import pallas as pl
from jax.experimental.pallas import tpu as pltpu
from jax.sharding import PartitionSpec as P

HEAD_DIM = 128
LANDMARKS = 512
ITERS = 3
ACROSS = ("z", "core")
PLANE = ("core", "space")
SCALE = 1.0 / math.sqrt(HEAD_DIM)
F32 = jnp.float32
BF16 = jnp.bfloat16


def softmax_rows(logits):
    ceiling = jnp.max(logits, axis=-1, keepdims=True)
    expo = jnp.exp(logits - ceiling)
    return expo / jnp.sum(expo, axis=-1, keepdims=True)


def halves(x):
    high = x.astype(BF16)
    return high, (x - high.astype(F32)).astype(BF16)


def triple(left, right):
    lh, ll = left
    rh, rl = right
    out = jnp.dot(lh, rh, preferred_element_type=F32)
    out += jnp.dot(lh, rl, preferred_element_type=F32)
    return out + jnp.dot(ll, rh, preferred_element_type=F32)


def inverse_body(q_ref, k_ref, high_ref, low_ref, out_ref, kh_ref, kl_ref):
    dims = (((1,), (1,)), ((), ()))
    q, k = q_ref[...], k_ref[...]
    logits = lax.dot_general(q, k, dims, preferred_element_type=F32) * SCALE
    kernel = softmax_rows(logits)
    column_top = jnp.max(jnp.sum(kernel, axis=0, keepdims=True))
    kh_ref[...], kl_ref[...] = halves(kernel)
    logits = lax.dot_general(k, q, dims, preferred_element_type=F32) * SCALE
    expo = jnp.exp(logits - jnp.max(logits, axis=0, keepdims=True))
    out_ref[...] = expo / (jnp.sum(expo, axis=0, keepdims=True) * column_top)

    def step(_, carry):
        iterate = out_ref[...]
        z = halves(iterate)
        y = halves(triple((kh_ref[...], kl_ref[...]), z))
        first = triple(z, y)
        second = triple(halves(first), y)
        third = triple(halves(second), y)
        out_ref[...] = 0.25 * (13.0 * iterate - 15.0 * first + 7.0 * second - third)
        return carry

    lax.fori_loop(0, ITERS, step, 0)
    high_ref[...], low_ref[...] = halves(out_ref[...])


def pseudo_inverse(q_land, k_land):
    whole = pl.BlockSpec(memory_space=pltpu.VMEM)
    return pl.pallas_call(
        inverse_body,
        out_shape=[jax.ShapeDtypeStruct((LANDMARKS, LANDMARKS), BF16)] * 2,
        in_specs=[whole, whole],
        out_specs=[whole, whole],
        scratch_shapes=[pltpu.VMEM((LANDMARKS, LANDMARKS), F32)]
        + [pltpu.VMEM((LANDMARKS, LANDMARKS), BF16)] * 2,
        compiler_params=pltpu.CompilerParams(vmem_limit_bytes=32 * 2**20),
        cost_estimate=pl.CostEstimate(
            flops=12 * 3 * 2 * LANDMARKS**3, bytes_accessed=2 * 2**20, transcendentals=0
        ),
    )(q_land, k_land)


def pack_body(q_ref, k_ref, v_ref, id_ref, out_ref):
    sides, part = id_ref.shape
    quad = out_ref.shape[0] // sides
    row = lax.broadcasted_iota(jnp.int32, (16, part), 0)
    for side in range(sides):
        ids = id_ref[side : side + 1, :]
        coarse = lax.shift_right_logical(ids, 8)
        fine = ids - coarse * 256
        tile = jnp.where(row == 0, coarse, jnp.where(row == 1, fine, 0))
        tile = tile.astype(F32).astype(BF16)
        rows = slice(side * part, (side + 1) * part)
        for head in range(quad):
            lanes = slice(head * HEAD_DIM, (head + 1) * HEAD_DIM)
            chunk = head * sides + side
            out_ref[chunk, :part, :] = q_ref[rows, lanes]
            out_ref[chunk, part : 2 * part, :] = k_ref[rows, lanes]
            out_ref[chunk, 2 * part : 3 * part, :] = v_ref[rows, lanes]
            out_ref[chunk, 3 * part : 3 * part + 16, :] = tile


def pack(queries, keys, values, groups, sides):
    count, width = queries.shape
    part = count // sides
    quad = 4
    columns = quad * HEAD_DIM
    cut = pl.BlockSpec((count, columns), lambda i: (0, i))
    rows = 3 * part + 16
    chunks = width // HEAD_DIM * sides
    return pl.pallas_call(
        pack_body,
        grid=(width // columns,),
        out_shape=jax.ShapeDtypeStruct((chunks, rows, HEAD_DIM), BF16),
        in_specs=[cut, cut, cut, pl.BlockSpec((sides, part), lambda i: (0, 0))],
        out_specs=pl.BlockSpec((quad * sides, rows, HEAD_DIM), lambda i: (i, 0, 0)),
        compiler_params=pltpu.CompilerParams(vmem_limit_bytes=56 * 2**20),
    )(queries, keys, values, groups.reshape(sides, part))


def unpack_body(in_ref, out_ref):
    chunks, part, _ = in_ref.shape
    sides = out_ref.shape[0] // part
    for chunk in range(chunks):
        head, side = chunk // sides, chunk % sides
        rows = slice(side * part, (side + 1) * part)
        out_ref[rows, head * HEAD_DIM : (head + 1) * HEAD_DIM] = in_ref[chunk]


def unpack(x, sides):
    chunks, part, _ = x.shape
    quad = 4
    return pl.pallas_call(
        unpack_body,
        grid=(chunks // sides // quad,),
        out_shape=jax.ShapeDtypeStruct((sides * part, chunks // sides * HEAD_DIM), BF16),
        in_specs=[pl.BlockSpec((quad * sides, part, HEAD_DIM), lambda i: (i, 0, 0))],
        out_specs=pl.BlockSpec((sides * part, quad * HEAD_DIM), lambda i: (0, i)),
        compiler_params=pltpu.CompilerParams(vmem_limit_bytes=24 * 2**20),
    )(x)


def local_call(body, out_shape, operands, megabytes, scratch=(), flops=0):
    whole = pl.BlockSpec(memory_space=pltpu.VMEM)
    size = sum(x.size * x.dtype.itemsize for x in operands)
    return pl.pallas_call(
        body,
        out_shape=out_shape,
        in_specs=[whole] * len(operands),
        out_specs=whole,
        scratch_shapes=list(scratch),
        compiler_params=pltpu.CompilerParams(vmem_limit_bytes=megabytes * 2**20),
        cost_estimate=pl.CostEstimate(flops=flops, bytes_accessed=size, transcendentals=0),
    )(*operands)


def sums_body(got_ref, out_ref, acc_ref):
    steps = got_ref.shape[0]
    part = (got_ref.shape[1] - 16) // 3
    plane, pair, _ = out_ref.shape
    block = pair // 2
    several = 4
    rows = lax.broadcasted_iota(jnp.int32, (LANDMARKS, part), 0)
    acc_ref[...] = jnp.zeros_like(acc_ref)

    def step(turn, carry):
        onehot, rest = [], []
        for inner in range(several):
            frame = turn * several + inner
            ids = got_ref[frame, 3 * part : 3 * part + 16, :].astype(F32)
            member = (ids[0:1, :] * 256.0 + ids[1:2, :]).astype(jnp.int32)
            onehot.append((rows == member).astype(F32).astype(BF16))
            rest.append(
                jnp.concatenate(
                    [got_ref[frame, :part, :], got_ref[frame, part : 2 * part, :]], axis=1
                )
            )
        acc_ref[...] += jnp.dot(
            jnp.concatenate(onehot, axis=1),
            jnp.concatenate(rest, axis=0),
            preferred_element_type=F32,
        )
        return carry

    lax.fori_loop(0, steps // several, step, 0)
    for side in range(2):
        x = acc_ref[:, side * HEAD_DIM : (side + 1) * HEAD_DIM].astype(BF16)
        out_ref[:, side * block : (side + 1) * block, :] = x.reshape(plane, block, HEAD_DIM)


def group_sums(got, plane):
    pair = 2 * LANDMARKS // plane
    return local_call(
        sums_body,
        jax.ShapeDtypeStruct((plane, pair, HEAD_DIM), BF16),
        [got],
        24,
        [pltpu.VMEM((LANDMARKS, 2 * HEAD_DIM), F32)],
        flops=4 * LANDMARKS * 4096 * HEAD_DIM,
    )


def combine_body(parts_ref, out_ref):
    x = parts_ref[...].astype(F32)
    tops = x[:, :, HEAD_DIM : HEAD_DIM + 1]
    totals = x[:, :, HEAD_DIM + 1 : HEAD_DIM + 2] + x[:, :, HEAD_DIM + 2 : HEAD_DIM + 3]
    factor = jnp.exp(tops - jnp.max(tops, axis=0, keepdims=True))
    weighted = jnp.sum(x[:, :, :HEAD_DIM] * factor, axis=0, keepdims=True)
    total = jnp.sum(totals * factor, axis=0, keepdims=True)
    out_ref[...] = jnp.broadcast_to((weighted / total).astype(BF16), out_ref.shape)


def combine(parts):
    plane, block, _ = parts.shape
    return local_call(
        combine_body, jax.ShapeDtypeStruct((plane, block, HEAD_DIM), BF16), [parts], 16
    )


def attend_body(got_ref, land_ref, out_ref):
    steps = got_ref.shape[0]
    part = (got_ref.shape[1] - 16) // 3
    several = 4
    land = land_ref[...]

    def step(turn, carry):
        tile = got_ref[pl.ds(turn * several, several), :part, :].reshape(several * part, HEAD_DIM)
        logits = lax.dot_general(
            tile, land, (((1,), (1,)), ((), ())), preferred_element_type=F32
        )
        logits = logits * SCALE
        expo = jnp.exp(logits - jnp.max(logits, axis=1, keepdims=True))
        weights = expo / jnp.sum(expo, axis=1, keepdims=True)
        start = pl.multiple_of(turn * several * part, several * part)
        out_ref[pl.ds(start, several * part), :] = weights.astype(BF16)
        return carry

    lax.fori_loop(0, steps // several, step, 0)


def token_weights(got, k_land):
    steps, rows, _ = got.shape
    tokens = steps * ((rows - 16) // 3)
    return local_call(
        attend_body,
        jax.ShapeDtypeStruct((tokens, LANDMARKS), BF16),
        [got, k_land],
        24,
        flops=2 * LANDMARKS * tokens * HEAD_DIM * 4,
    )


def final_body(high_ref, low_ref, summary_ref, attend_ref, temporal_ref, out_ref):
    steps, part, _ = out_ref.shape
    several = 4
    summary = summary_ref[...].reshape(LANDMARKS, HEAD_DIM)
    mixed = jnp.dot(high_ref[...], summary, preferred_element_type=F32)
    mixed += jnp.dot(low_ref[...], summary, preferred_element_type=F32)
    mixed = mixed.astype(BF16)

    def step(turn, carry):
        start = pl.multiple_of(turn * several * part, several * part)
        rows = pl.ds(start, several * part)
        tile = jnp.dot(attend_ref[rows, :], mixed, preferred_element_type=F32)
        tile = (tile + temporal_ref[rows, :].astype(F32)).astype(BF16)
        out_ref[pl.ds(turn * several, several)] = tile.reshape(several, part, HEAD_DIM)
        return carry

    lax.fori_loop(0, steps // several, step, 0)


def finish(high, low, summary, attend, temporal, steps, part):
    return local_call(
        final_body,
        jax.ShapeDtypeStruct((steps, part, HEAD_DIM), BF16),
        [high, low, summary, attend, temporal],
        24,
        flops=4 * LANDMARKS * steps * part * HEAD_DIM,
    )


def swap(x, axes):
    return lax.all_to_all(x, axes, split_axis=0, concat_axis=0, tiled=True)


def share(x, axes):
    size = lax.axis_size(axes)
    return swap(jnp.broadcast_to(x[None], (size,) + x.shape), axes)


def local(queries, keys, values, groups):
    frames, count, width = queries.shape
    heads = width // HEAD_DIM
    sides = lax.axis_size("core")
    steps = heads * sides
    part = count // sides
    tokens = steps * part
    plane = lax.axis_size(PLANE)
    block = LANDMARKS // plane

    packed = pack(queries[0], keys[0], values[0], groups, sides)
    got = swap(packed, ACROSS)
    q = got[:, :part].reshape(tokens, HEAD_DIM)
    k = got[:, part : 2 * part].reshape(tokens, HEAD_DIM)
    v = got[:, 2 * part : 3 * part].reshape(tokens, HEAD_DIM)
    members_each = plane * tokens // LANDMARKS
    sums = jnp.sum(swap(group_sums(got, plane), PLANE).astype(F32), axis=0)
    lands = share((sums / members_each).astype(BF16), PLANE)
    q_land = lands[:, :block].reshape(LANDMARKS, HEAD_DIM)
    k_land = lands[:, block:].reshape(LANDMARKS, HEAD_DIM)

    few = 8

    def split(x):
        x = x.reshape(steps, part // few, few, HEAD_DIM)
        return jnp.swapaxes(x, 0, 1).reshape(part // few, steps * few, HEAD_DIM)

    logits = jnp.einsum("sae,sbe->sab", split(q), split(k), preferred_element_type=F32) * SCALE
    index = jnp.arange(steps * few, dtype=jnp.int32) % few
    logits = jnp.where(index[:, None] == index[None, :], logits, -jnp.inf)
    weights = softmax_rows(logits).astype(BF16)
    temporal = jnp.einsum("sab,sbe->sae", weights, split(v), preferred_element_type=F32)
    temporal = temporal.astype(BF16).reshape(part // few, steps, few, HEAD_DIM)
    temporal = jnp.swapaxes(temporal, 0, 1).reshape(tokens, HEAD_DIM)

    land_logits = jnp.einsum("me,se->ms", q_land, k, preferred_element_type=F32) * SCALE
    own_top = jnp.max(land_logits, axis=-1, keepdims=True).astype(BF16)
    own_weights = jnp.exp(land_logits - own_top.astype(F32))
    own_total = jnp.sum(own_weights, axis=-1, keepdims=True)
    own_sum = jnp.dot(own_weights.astype(BF16), temporal, preferred_element_type=F32)
    high, low = halves(own_total)
    extra = jnp.pad(
        jnp.concatenate([own_top, high, low], axis=1), ((0, 0), (0, HEAD_DIM - 3))
    )
    own = jnp.concatenate([own_sum.astype(BF16), extra], axis=1)
    high, low = pseudo_inverse(q_land, k_land)
    parts = swap(own.reshape(plane, block, 2 * HEAD_DIM), PLANE)
    parts, high, low = lax.optimization_barrier((parts, high, low))
    summary = swap(combine(parts), PLANE)
    attend = token_weights(got, k_land)
    out = finish(high, low, summary, attend, temporal, steps, part)
    back = swap(out, ACROSS)
    return unpack(back, sides)[None]


def solution(mesh):
    tm, space = mesh.devices.shape
    fine = jax.sharding.Mesh(mesh.devices.reshape(tm // 2, 2, space), ("z", "core", "space"))
    block = P(("z", "core"), "space", None)
    return jax.shard_map(
        local,
        mesh=fine,
        in_specs=(block, block, block, P(("z", "core"), "space")),
        out_specs=block,
        check_vma=False,
    )
```

```python
import math

import jax
import jax.numpy as jnp
from jax import lax
from jax.experimental import pallas as pl
from jax.experimental.pallas import tpu as pltpu
from jax.sharding import PartitionSpec as P

HEAD_DIM = 128
LANDMARKS = 512
ITERS = 3
GROUP = 256
ACROSS = ("z", "core")
PLANE = ("core", "space")
SCALE = 1.0 / math.sqrt(HEAD_DIM)
F32 = jnp.float32
BF16 = jnp.bfloat16


def softmax_rows(logits):
    ceiling = jnp.max(logits, axis=-1, keepdims=True)
    expo = jnp.exp(logits - ceiling)
    return expo / jnp.sum(expo, axis=-1, keepdims=True)


def halves(x):
    high = x.astype(BF16)
    return high, (x - high.astype(F32)).astype(BF16)


def triple(left, right):
    lh, ll = left
    rh, rl = right
    return jnp.dot(
        jnp.concatenate([lh, lh, ll], axis=1),
        jnp.concatenate([rh, rl, rh], axis=0),
        preferred_element_type=F32,
    )


def newton(iterate, z, y):
    first = triple(z, y)
    second = triple(halves(first), y)
    third = triple(halves(second), y)
    return 0.25 * (13.0 * iterate - 15.0 * first + 7.0 * second - third)


def inverse_body(q_ref, k_ref, zh_ref, zl_ref, yh_ref, yl_ref, out_ref, kh_ref, kl_ref):
    dims = (((1,), (1,)), ((), ()))
    q, k = q_ref[...], k_ref[...]
    logits = lax.dot_general(q, k, dims, preferred_element_type=F32) * SCALE
    kernel = softmax_rows(logits)
    column_top = jnp.max(jnp.sum(kernel, axis=0, keepdims=True))
    kh_ref[...], kl_ref[...] = halves(kernel)
    logits = lax.dot_general(k, q, dims, preferred_element_type=F32) * SCALE
    expo = jnp.exp(logits - jnp.max(logits, axis=0, keepdims=True))
    out_ref[...] = expo / (jnp.sum(expo, axis=0, keepdims=True) * column_top)

    def step(_, carry):
        iterate = out_ref[...]
        z = halves(iterate)
        y = halves(triple((kh_ref[...], kl_ref[...]), z))
        out_ref[...] = newton(iterate, z, y)
        return carry

    lax.fori_loop(0, ITERS - 1, step, 0)
    z = halves(out_ref[...])
    zh_ref[...], zl_ref[...] = z
    yh_ref[...], yl_ref[...] = halves(triple((kh_ref[...], kl_ref[...]), z))


def whole_call(body, out_shape, operands, megabytes, scratch=(), flops=0):
    size = sum(x.size * x.dtype.itemsize for x in operands)
    return pl.pallas_call(
        body,
        out_shape=out_shape,
        scratch_shapes=list(scratch),
        compiler_params=pltpu.CompilerParams(vmem_limit_bytes=megabytes * 2**20),
        cost_estimate=pl.CostEstimate(flops=flops, bytes_accessed=size, transcendentals=0),
    )(*operands)


def inverse_parts(q_land, k_land):
    return whole_call(
        inverse_body,
        [jax.ShapeDtypeStruct((LANDMARKS, LANDMARKS), BF16)] * 4,
        [q_land, k_land],
        24,
        [pltpu.VMEM((LANDMARKS, LANDMARKS), F32)] + [pltpu.VMEM((LANDMARKS, LANDMARKS), BF16)] * 2,
        flops=9 * 3 * 2 * LANDMARKS**3,
    )


def last_body(zh_ref, zl_ref, yh_ref, yl_ref, high_ref, low_ref):
    z = (zh_ref[...], zl_ref[...])
    y = (yh_ref[...], yl_ref[...])
    iterate = z[0].astype(F32) + z[1].astype(F32)
    high_ref[...], low_ref[...] = halves(newton(iterate, z, y))


def last_iteration(parts):
    return whole_call(
        last_body,
        [jax.ShapeDtypeStruct((LANDMARKS, LANDMARKS), BF16)] * 2,
        list(parts),
        24,
        flops=3 * 3 * 2 * LANDMARKS**3,
    )


def pack_body(q_ref, k_ref, v_ref, id_ref, out_ref):
    sides, part = id_ref.shape
    quad = out_ref.shape[0] // sides
    row = lax.broadcasted_iota(jnp.int32, (16, part), 0)
    for side in range(sides):
        ids = id_ref[side : side + 1, :]
        coarse = lax.shift_right_logical(ids, 8)
        fine = ids - coarse * 256
        tile = jnp.where(row == 0, coarse, jnp.where(row == 1, fine, 0))
        tile = tile.astype(F32).astype(BF16)
        rows = slice(side * part, (side + 1) * part)
        for head in range(quad):
            lanes = slice(head * HEAD_DIM, (head + 1) * HEAD_DIM)
            chunk = head * sides + side
            out_ref[chunk, :part, :] = q_ref[rows, lanes]
            out_ref[chunk, part : 2 * part, :] = k_ref[rows, lanes]
            out_ref[chunk, 2 * part : 3 * part, :] = v_ref[rows, lanes]
            out_ref[chunk, 3 * part : 3 * part + 16, :] = tile


def pack(queries, keys, values, groups, sides):
    count, width = queries.shape
    part = count // sides
    quad = 4
    columns = quad * HEAD_DIM
    cut = pl.BlockSpec((count, columns), lambda i: (0, i))
    rows = 3 * part + 16
    chunks = width // HEAD_DIM * sides
    return pl.pallas_call(
        pack_body,
        grid=(width // columns,),
        out_shape=jax.ShapeDtypeStruct((chunks, rows, HEAD_DIM), BF16),
        in_specs=[cut, cut, cut, pl.BlockSpec((sides, part), lambda i: (0, 0))],
        out_specs=pl.BlockSpec((quad * sides, rows, HEAD_DIM), lambda i: (i, 0, 0)),
        compiler_params=pltpu.CompilerParams(vmem_limit_bytes=12 * 2**20),
    )(queries, keys, values, groups.reshape(sides, part))


def unpack_body(in_ref, out_ref):
    chunks, part, _ = in_ref.shape
    sides = out_ref.shape[0] // part
    for chunk in range(chunks):
        head, side = chunk // sides, chunk % sides
        rows = slice(side * part, (side + 1) * part)
        out_ref[rows, head * HEAD_DIM : (head + 1) * HEAD_DIM] = in_ref[chunk]


def unpack(x, sides):
    chunks, part, _ = x.shape
    quad = 4
    return pl.pallas_call(
        unpack_body,
        grid=(chunks // sides // quad,),
        out_shape=jax.ShapeDtypeStruct((sides * part, chunks // sides * HEAD_DIM), BF16),
        in_specs=[pl.BlockSpec((quad * sides, part, HEAD_DIM), lambda i: (i, 0, 0))],
        out_specs=pl.BlockSpec((sides * part, quad * HEAD_DIM), lambda i: (0, i)),
        compiler_params=pltpu.CompilerParams(vmem_limit_bytes=12 * 2**20),
    )(x)


def sums_body(got_ref, out_ref, acc_ref):
    several = got_ref.shape[0]
    part = (got_ref.shape[1] - 16) // 3
    plane, pair, _ = out_ref.shape
    block = pair // 2
    turn = pl.program_id(0)

    @pl.when(turn == 0)
    def _():
        acc_ref[...] = jnp.zeros_like(acc_ref)

    rows = lax.broadcasted_iota(jnp.int32, (LANDMARKS, part), 0)
    onehot, rest = [], []
    for frame in range(several):
        ids = got_ref[frame, 3 * part : 3 * part + 16, :].astype(F32)
        member = (ids[0:1, :] * 256.0 + ids[1:2, :]).astype(jnp.int32)
        onehot.append((rows == member).astype(F32).astype(BF16))
        rest.append(
            jnp.concatenate([got_ref[frame, :part, :], got_ref[frame, part : 2 * part, :]], axis=1)
        )
    acc_ref[...] += jnp.dot(
        jnp.concatenate(onehot, axis=1),
        jnp.concatenate(rest, axis=0),
        preferred_element_type=F32,
    )

    @pl.when(turn == pl.num_programs(0) - 1)
    def _():
        for side in range(2):
            x = acc_ref[:, side * HEAD_DIM : (side + 1) * HEAD_DIM].astype(BF16)
            out_ref[:, side * block : (side + 1) * block, :] = x.reshape(plane, block, HEAD_DIM)


def group_sums(got, plane):
    steps, rows, _ = got.shape
    several = 4
    pair = 2 * LANDMARKS // plane
    return pl.pallas_call(
        sums_body,
        grid=(steps // several,),
        out_shape=jax.ShapeDtypeStruct((plane, pair, HEAD_DIM), BF16),
        in_specs=[pl.BlockSpec((several, rows, HEAD_DIM), lambda i: (i, 0, 0))],
        out_specs=pl.BlockSpec((plane, pair, HEAD_DIM), lambda i: (0, 0, 0)),
        scratch_shapes=[pltpu.VMEM((LANDMARKS, 2 * HEAD_DIM), F32)],
        compiler_params=pltpu.CompilerParams(vmem_limit_bytes=12 * 2**20),
    )(got)


def mean_body(parts_ref, out_ref):
    total = jnp.sum(parts_ref[...].astype(F32), axis=0, keepdims=True)
    mean = (total / GROUP).astype(BF16)
    out_ref[...] = jnp.broadcast_to(mean, out_ref.shape)


def group_means(parts):
    return whole_call(mean_body, jax.ShapeDtypeStruct(parts.shape, BF16), [parts], 8)


def combine_body(parts_ref, out_ref):
    x = parts_ref[...].astype(F32)
    tops = x[:, :, HEAD_DIM : HEAD_DIM + 1]
    totals = x[:, :, HEAD_DIM + 1 : HEAD_DIM + 2] + x[:, :, HEAD_DIM + 2 : HEAD_DIM + 3]
    factor = jnp.exp(tops - jnp.max(tops, axis=0, keepdims=True))
    weighted = jnp.sum(x[:, :, :HEAD_DIM] * factor, axis=0, keepdims=True)
    total = jnp.sum(totals * factor, axis=0, keepdims=True)
    out_ref[...] = jnp.broadcast_to((weighted / total).astype(BF16), out_ref.shape)


def combine(parts):
    plane, block, _ = parts.shape
    return whole_call(
        combine_body, jax.ShapeDtypeStruct((plane, block, HEAD_DIM), BF16), [parts], 8
    )


def attend_body(tile_ref, land_ref, out_ref):
    tile = tile_ref[...].reshape(out_ref.shape[0], HEAD_DIM)
    logits = lax.dot_general(
        tile, land_ref[...], (((1,), (1,)), ((), ())), preferred_element_type=F32
    )
    logits = logits * SCALE
    expo = jnp.exp(logits - jnp.max(logits, axis=1, keepdims=True))
    out_ref[...] = (expo / jnp.sum(expo, axis=1, keepdims=True)).astype(BF16)


def token_weights(got, k_land):
    steps, rows, _ = got.shape
    part = (rows - 16) // 3
    several = 4
    return pl.pallas_call(
        attend_body,
        grid=(steps // several,),
        out_shape=jax.ShapeDtypeStruct((steps * part, LANDMARKS), BF16),
        in_specs=[
            pl.BlockSpec((several, part, HEAD_DIM), lambda i: (i, 0, 0)),
            pl.BlockSpec((LANDMARKS, HEAD_DIM), lambda i: (0, 0)),
        ],
        out_specs=pl.BlockSpec((several * part, LANDMARKS), lambda i: (i, 0)),
        compiler_params=pltpu.CompilerParams(vmem_limit_bytes=12 * 2**20),
        cost_estimate=pl.CostEstimate(
            flops=8 * LANDMARKS * steps * part * HEAD_DIM,
            bytes_accessed=5 * 2**20,
            transcendentals=0,
        ),
    )(got, k_land)


def final_body(high_ref, low_ref, summary_ref, attend_ref, temporal_ref, out_ref, mixed_ref):
    @pl.when(pl.program_id(0) == 0)
    def _():
        summary = summary_ref[...].reshape(LANDMARKS, HEAD_DIM)
        mixed = jnp.dot(high_ref[...], summary, preferred_element_type=F32)
        mixed += jnp.dot(low_ref[...], summary, preferred_element_type=F32)
        mixed_ref[...] = mixed.astype(BF16)

    tile = jnp.dot(attend_ref[...], mixed_ref[...], preferred_element_type=F32)
    tile = (tile + temporal_ref[...].astype(F32)).astype(BF16)
    out_ref[...] = tile.reshape(out_ref.shape)


def finish(high, low, summary, attend, temporal, steps, part):
    several = 8
    square = pl.BlockSpec((LANDMARKS, LANDMARKS), lambda i: (0, 0))
    return pl.pallas_call(
        final_body,
        grid=(steps // several,),
        out_shape=jax.ShapeDtypeStruct((steps, part, HEAD_DIM), BF16),
        in_specs=[
            square,
            square,
            pl.BlockSpec(summary.shape, lambda i: (0, 0, 0)),
            pl.BlockSpec((several * part, LANDMARKS), lambda i: (i, 0)),
            pl.BlockSpec((several * part, HEAD_DIM), lambda i: (i, 0)),
        ],
        out_specs=pl.BlockSpec((several, part, HEAD_DIM), lambda i: (i, 0, 0)),
        scratch_shapes=[pltpu.VMEM((LANDMARKS, HEAD_DIM), BF16)],
        compiler_params=pltpu.CompilerParams(vmem_limit_bytes=16 * 2**20),
    )(high, low, summary, attend, temporal)


def swap(x, axes):
    return lax.all_to_all(x, axes, split_axis=0, concat_axis=0, tiled=True)


def local(queries, keys, values, groups):
    frames, count, width = queries.shape
    heads = width // HEAD_DIM
    sides = lax.axis_size("core")
    steps = heads * sides
    part = count // sides
    tokens = steps * part
    plane = lax.axis_size(PLANE)
    block = LANDMARKS // plane

    packed = pack(queries[0], keys[0], values[0], groups, sides)
    got = swap(packed, ACROSS)
    q = got[:, :part].reshape(tokens, HEAD_DIM)
    k = got[:, part : 2 * part].reshape(tokens, HEAD_DIM)
    v = got[:, 2 * part : 3 * part].reshape(tokens, HEAD_DIM)
    lands = swap(group_means(swap(group_sums(got, plane), PLANE)), PLANE)
    q_land = lands[:, :block].reshape(LANDMARKS, HEAD_DIM)
    k_land = lands[:, block:].reshape(LANDMARKS, HEAD_DIM)

    few = 8

    def split(x):
        x = x.reshape(steps, part // few, few, HEAD_DIM)
        return jnp.swapaxes(x, 0, 1).reshape(part // few, steps * few, HEAD_DIM)

    logits = jnp.einsum("sae,sbe->sab", split(q), split(k), preferred_element_type=F32) * SCALE
    index = jnp.arange(steps * few, dtype=jnp.int32) % few
    logits = jnp.where(index[:, None] == index[None, :], logits, -jnp.inf)
    weights = softmax_rows(logits).astype(BF16)
    temporal = jnp.einsum("sab,sbe->sae", weights, split(v), preferred_element_type=F32)
    temporal = temporal.astype(BF16).reshape(part // few, steps, few, HEAD_DIM)
    temporal = jnp.swapaxes(temporal, 0, 1).reshape(tokens, HEAD_DIM)

    land_logits = jnp.einsum("me,se->ms", q_land, k, preferred_element_type=F32) * SCALE
    own_top = jnp.max(land_logits, axis=-1, keepdims=True).astype(BF16)
    own_weights = jnp.exp(land_logits - own_top.astype(F32))
    own_total = jnp.sum(own_weights, axis=-1, keepdims=True)
    own_sum = jnp.dot(own_weights.astype(BF16), temporal, preferred_element_type=F32)
    high, low = halves(own_total)
    extra = jnp.pad(
        jnp.concatenate([own_top, high, low], axis=1), ((0, 0), (0, HEAD_DIM - 3))
    )
    own = jnp.concatenate([own_sum.astype(BF16), extra], axis=1)
    inverse = inverse_parts(q_land, k_land)
    parts = swap(own.reshape(plane, block, 2 * HEAD_DIM), PLANE)
    parts, inverse = lax.optimization_barrier((parts, inverse))
    summary = swap(combine(parts), PLANE)
    attend = token_weights(got, k_land)
    high, low = last_iteration(inverse)
    out = finish(high, low, summary, attend, temporal, steps, part)
    back = swap(out, ACROSS)
    return unpack(back, sides)[None]


def solution(mesh):
    tm, space = mesh.devices.shape
    fine = jax.sharding.Mesh(mesh.devices.reshape(tm // 2, 2, space), ("z", "core", "space"))
    block = P(("z", "core"), "space", None)
    return jax.shard_map(
        local,
        mesh=fine,
        in_specs=(block, block, block, P(("z", "core"), "space")),
        out_specs=block,
        check_vma=False,
    )
```

```python
import math

import jax
import jax.numpy as jnp
from jax import lax
from jax.experimental import pallas as pl
from jax.experimental.pallas import tpu as pltpu
from jax.sharding import PartitionSpec as P

HEAD_DIM = 128
LANDMARKS = 512
ITERS = 3
GROUP = 256
ACROSS = ("z", "core")
PLANE = ("core", "space")
SCALE = 1.0 / math.sqrt(HEAD_DIM)
F32 = jnp.float32
BF16 = jnp.bfloat16


def softmax_rows(logits):
    ceiling = jnp.max(logits, axis=-1, keepdims=True)
    expo = jnp.exp(logits - ceiling)
    return expo / jnp.sum(expo, axis=-1, keepdims=True)


def in_hbm(*arrays):
    return [pltpu.with_memory_space_constraint(x, pltpu.HBM) for x in arrays]


def halves(x):
    high = x.astype(BF16)
    return high, (x - high.astype(F32)).astype(BF16)


def triple(left, right):
    lh, ll = left
    rh, rl = right
    return jnp.dot(
        jnp.concatenate([lh, lh, ll], axis=1),
        jnp.concatenate([rh, rl, rh], axis=0),
        preferred_element_type=F32,
    )


def newton(iterate, z, y):
    first = triple(z, y)
    second = triple(halves(first), y)
    third = triple(halves(second), y)
    return 0.25 * (13.0 * iterate - 15.0 * first + 7.0 * second - third)


def inverse_body(q_ref, k_ref, zh_ref, zl_ref, yh_ref, yl_ref, out_ref, kh_ref, kl_ref):
    dims = (((1,), (1,)), ((), ()))
    q, k = q_ref[...], k_ref[...]
    logits = lax.dot_general(q, k, dims, preferred_element_type=F32) * SCALE
    kernel = softmax_rows(logits)
    column_top = jnp.max(jnp.sum(kernel, axis=0, keepdims=True))
    kh_ref[...], kl_ref[...] = halves(kernel)
    logits = lax.dot_general(k, q, dims, preferred_element_type=F32) * SCALE
    expo = jnp.exp(logits - jnp.max(logits, axis=0, keepdims=True))
    out_ref[...] = expo / (jnp.sum(expo, axis=0, keepdims=True) * column_top)

    def step(_, carry):
        iterate = out_ref[...]
        z = halves(iterate)
        y = halves(triple((kh_ref[...], kl_ref[...]), z))
        out_ref[...] = newton(iterate, z, y)
        return carry

    lax.fori_loop(0, ITERS - 1, step, 0)
    z = halves(out_ref[...])
    zh_ref[...], zl_ref[...] = z
    yh_ref[...], yl_ref[...] = halves(triple((kh_ref[...], kl_ref[...]), z))


def whole_call(body, out_shape, operands, megabytes, scratch=(), flops=0):
    size = sum(x.size * x.dtype.itemsize for x in operands)
    return pl.pallas_call(
        body,
        out_shape=out_shape,
        scratch_shapes=list(scratch),
        compiler_params=pltpu.CompilerParams(vmem_limit_bytes=megabytes * 2**20),
        cost_estimate=pl.CostEstimate(flops=flops, bytes_accessed=size, transcendentals=0),
    )(*operands)


def inverse_parts(q_land, k_land):
    return whole_call(
        inverse_body,
        [pltpu.HBM((LANDMARKS, LANDMARKS), BF16)] * 4,
        in_hbm(q_land, k_land),
        24,
        [pltpu.VMEM((LANDMARKS, LANDMARKS), F32)] + [pltpu.VMEM((LANDMARKS, LANDMARKS), BF16)] * 2,
        flops=9 * 3 * 2 * LANDMARKS**3,
    )


def last_body(zh_ref, zl_ref, yh_ref, yl_ref, high_ref, low_ref):
    z = (zh_ref[...], zl_ref[...])
    y = (yh_ref[...], yl_ref[...])
    iterate = z[0].astype(F32) + z[1].astype(F32)
    high_ref[...], low_ref[...] = halves(newton(iterate, z, y))


def last_iteration(parts):
    return whole_call(
        last_body,
        [pltpu.HBM((LANDMARKS, LANDMARKS), BF16)] * 2,
        in_hbm(*parts),
        24,
        flops=3 * 3 * 2 * LANDMARKS**3,
    )


def pack_body(q_ref, k_ref, v_ref, id_ref, out_ref):
    sides, part = id_ref.shape
    quad = out_ref.shape[0] // sides
    row = lax.broadcasted_iota(jnp.int32, (16, part), 0)
    for side in range(sides):
        ids = id_ref[side : side + 1, :]
        coarse = lax.shift_right_logical(ids, 8)
        fine = ids - coarse * 256
        tile = jnp.where(row == 0, coarse, jnp.where(row == 1, fine, 0))
        tile = tile.astype(F32).astype(BF16)
        rows = slice(side * part, (side + 1) * part)
        for head in range(quad):
            lanes = slice(head * HEAD_DIM, (head + 1) * HEAD_DIM)
            chunk = head * sides + side
            out_ref[chunk, :part, :] = q_ref[rows, lanes]
            out_ref[chunk, part : 2 * part, :] = k_ref[rows, lanes]
            out_ref[chunk, 2 * part : 3 * part, :] = v_ref[rows, lanes]
            out_ref[chunk, 3 * part : 3 * part + 16, :] = tile


def pack(queries, keys, values, groups, sides):
    count, width = queries.shape
    part = count // sides
    quad = 4
    columns = quad * HEAD_DIM
    cut = pl.BlockSpec((count, columns), lambda i: (0, i))
    rows = 3 * part + 16
    chunks = width // HEAD_DIM * sides
    return pl.pallas_call(
        pack_body,
        grid=(width // columns,),
        out_shape=pltpu.HBM((chunks, rows, HEAD_DIM), BF16),
        in_specs=[cut, cut, cut, pl.BlockSpec((sides, part), lambda i: (0, 0))],
        out_specs=pl.BlockSpec((quad * sides, rows, HEAD_DIM), lambda i: (i, 0, 0)),
        compiler_params=pltpu.CompilerParams(vmem_limit_bytes=12 * 2**20),
    )(*in_hbm(queries, keys, values, groups.reshape(sides, part)))


def unpack_body(in_ref, out_ref):
    chunks, part, _ = in_ref.shape
    sides = out_ref.shape[0] // part
    for chunk in range(chunks):
        head, side = chunk // sides, chunk % sides
        rows = slice(side * part, (side + 1) * part)
        out_ref[rows, head * HEAD_DIM : (head + 1) * HEAD_DIM] = in_ref[chunk]


def unpack(x, sides):
    chunks, part, _ = x.shape
    quad = 4
    return pl.pallas_call(
        unpack_body,
        grid=(chunks // sides // quad,),
        out_shape=jax.ShapeDtypeStruct((sides * part, chunks // sides * HEAD_DIM), BF16),
        in_specs=[pl.BlockSpec((quad * sides, part, HEAD_DIM), lambda i: (i, 0, 0))],
        out_specs=pl.BlockSpec((sides * part, quad * HEAD_DIM), lambda i: (0, i)),
        compiler_params=pltpu.CompilerParams(vmem_limit_bytes=12 * 2**20),
    )(x)


def sums_body(got_ref, out_ref, acc_ref):
    several = got_ref.shape[0]
    part = (got_ref.shape[1] - 16) // 3
    plane, pair, _ = out_ref.shape
    block = pair // 2
    turn = pl.program_id(0)

    @pl.when(turn == 0)
    def _():
        acc_ref[...] = jnp.zeros_like(acc_ref)

    rows = lax.broadcasted_iota(jnp.int32, (LANDMARKS, part), 0)
    onehot, rest = [], []
    for frame in range(several):
        ids = got_ref[frame, 3 * part : 3 * part + 16, :].astype(F32)
        member = (ids[0:1, :] * 256.0 + ids[1:2, :]).astype(jnp.int32)
        onehot.append((rows == member).astype(F32).astype(BF16))
        rest.append(
            jnp.concatenate([got_ref[frame, :part, :], got_ref[frame, part : 2 * part, :]], axis=1)
        )
    acc_ref[...] += jnp.dot(
        jnp.concatenate(onehot, axis=1),
        jnp.concatenate(rest, axis=0),
        preferred_element_type=F32,
    )

    @pl.when(turn == pl.num_programs(0) - 1)
    def _():
        for side in range(2):
            x = acc_ref[:, side * HEAD_DIM : (side + 1) * HEAD_DIM].astype(BF16)
            out_ref[:, side * block : (side + 1) * block, :] = x.reshape(plane, block, HEAD_DIM)


def group_sums(got, plane):
    steps, rows, _ = got.shape
    several = 4
    pair = 2 * LANDMARKS // plane
    return pl.pallas_call(
        sums_body,
        grid=(steps // several,),
        out_shape=pltpu.HBM((plane, pair, HEAD_DIM), BF16),
        in_specs=[pl.BlockSpec((several, rows, HEAD_DIM), lambda i: (i, 0, 0))],
        out_specs=pl.BlockSpec((plane, pair, HEAD_DIM), lambda i: (0, 0, 0)),
        scratch_shapes=[pltpu.VMEM((LANDMARKS, 2 * HEAD_DIM), F32)],
        compiler_params=pltpu.CompilerParams(vmem_limit_bytes=12 * 2**20),
    )(got)


def mean_body(parts_ref, out_ref):
    total = jnp.sum(parts_ref[...].astype(F32), axis=0, keepdims=True)
    mean = (total / GROUP).astype(BF16)
    out_ref[...] = jnp.broadcast_to(mean, out_ref.shape)


def group_means(parts):
    return whole_call(mean_body, pltpu.HBM(parts.shape, BF16), [parts], 8)


def combine_body(parts_ref, out_ref):
    x = parts_ref[...].astype(F32)
    tops = x[:, :, HEAD_DIM : HEAD_DIM + 1]
    totals = x[:, :, HEAD_DIM + 1 : HEAD_DIM + 2] + x[:, :, HEAD_DIM + 2 : HEAD_DIM + 3]
    factor = jnp.exp(tops - jnp.max(tops, axis=0, keepdims=True))
    weighted = jnp.sum(x[:, :, :HEAD_DIM] * factor, axis=0, keepdims=True)
    total = jnp.sum(totals * factor, axis=0, keepdims=True)
    out_ref[...] = jnp.broadcast_to((weighted / total).astype(BF16), out_ref.shape)


def combine(parts):
    plane, block, _ = parts.shape
    return whole_call(
        combine_body, pltpu.HBM((plane, block, HEAD_DIM), BF16), [parts], 8
    )


def attend_body(tile_ref, land_ref, out_ref):
    tile = tile_ref[...].reshape(out_ref.shape[0], HEAD_DIM)
    logits = lax.dot_general(
        tile, land_ref[...], (((1,), (1,)), ((), ())), preferred_element_type=F32
    )
    logits = logits * SCALE
    expo = jnp.exp(logits - jnp.max(logits, axis=1, keepdims=True))
    out_ref[...] = (expo / jnp.sum(expo, axis=1, keepdims=True)).astype(BF16)


def token_weights(got, k_land):
    steps, rows, _ = got.shape
    part = (rows - 16) // 3
    several = 4
    return pl.pallas_call(
        attend_body,
        grid=(steps // several,),
        out_shape=pltpu.HBM((steps * part, LANDMARKS), BF16),
        in_specs=[
            pl.BlockSpec((several, part, HEAD_DIM), lambda i: (i, 0, 0)),
            pl.BlockSpec((LANDMARKS, HEAD_DIM), lambda i: (0, 0)),
        ],
        out_specs=pl.BlockSpec((several * part, LANDMARKS), lambda i: (i, 0)),
        compiler_params=pltpu.CompilerParams(vmem_limit_bytes=12 * 2**20),
        cost_estimate=pl.CostEstimate(
            flops=8 * LANDMARKS * steps * part * HEAD_DIM,
            bytes_accessed=5 * 2**20,
            transcendentals=0,
        ),
    )(got, *in_hbm(k_land))


def final_body(high_ref, low_ref, summary_ref, attend_ref, temporal_ref, out_ref, mixed_ref):
    @pl.when(pl.program_id(0) == 0)
    def _():
        summary = summary_ref[...].reshape(LANDMARKS, HEAD_DIM)
        mixed = jnp.dot(high_ref[...], summary, preferred_element_type=F32)
        mixed += jnp.dot(low_ref[...], summary, preferred_element_type=F32)
        mixed_ref[...] = mixed.astype(BF16)

    tile = jnp.dot(attend_ref[...], mixed_ref[...], preferred_element_type=F32)
    tile = (tile + temporal_ref[...].astype(F32)).astype(BF16)
    out_ref[...] = tile.reshape(out_ref.shape)


def finish(high, low, summary, attend, temporal, steps, part):
    several = 8
    square = pl.BlockSpec((LANDMARKS, LANDMARKS), lambda i: (0, 0))
    return pl.pallas_call(
        final_body,
        grid=(steps // several,),
        out_shape=jax.ShapeDtypeStruct((steps, part, HEAD_DIM), BF16),
        in_specs=[
            square,
            square,
            pl.BlockSpec(summary.shape, lambda i: (0, 0, 0)),
            pl.BlockSpec((several * part, LANDMARKS), lambda i: (i, 0)),
            pl.BlockSpec((several * part, HEAD_DIM), lambda i: (i, 0)),
        ],
        out_specs=pl.BlockSpec((several, part, HEAD_DIM), lambda i: (i, 0, 0)),
        scratch_shapes=[pltpu.VMEM((LANDMARKS, HEAD_DIM), BF16)],
        compiler_params=pltpu.CompilerParams(vmem_limit_bytes=16 * 2**20),
    )(*in_hbm(high, low), summary, *in_hbm(attend, temporal))


def swap(x, axes):
    return lax.all_to_all(x, axes, split_axis=0, concat_axis=0, tiled=True)


def local(queries, keys, values, groups):
    frames, count, width = queries.shape
    heads = width // HEAD_DIM
    sides = lax.axis_size("core")
    steps = heads * sides
    part = count // sides
    tokens = steps * part
    plane = lax.axis_size(PLANE)
    block = LANDMARKS // plane

    packed = pack(queries[0], keys[0], values[0], groups, sides)
    got = swap(packed, ACROSS)
    q = got[:, :part].reshape(tokens, HEAD_DIM)
    k = got[:, part : 2 * part].reshape(tokens, HEAD_DIM)
    v = got[:, 2 * part : 3 * part].reshape(tokens, HEAD_DIM)
    lands = swap(group_means(swap(group_sums(got, plane), PLANE)), PLANE)
    q_land = lands[:, :block].reshape(LANDMARKS, HEAD_DIM)
    k_land = lands[:, block:].reshape(LANDMARKS, HEAD_DIM)

    few = 8

    def split(x):
        x = x.reshape(steps, part // few, few, HEAD_DIM)
        return jnp.swapaxes(x, 0, 1).reshape(part // few, steps * few, HEAD_DIM)

    logits = jnp.einsum("sae,sbe->sab", split(q), split(k), preferred_element_type=F32) * SCALE
    index = jnp.arange(steps * few, dtype=jnp.int32) % few
    logits = jnp.where(index[:, None] == index[None, :], logits, -jnp.inf)
    weights = softmax_rows(logits).astype(BF16)
    temporal = jnp.einsum("sab,sbe->sae", weights, split(v), preferred_element_type=F32)
    temporal = temporal.astype(BF16).reshape(part // few, steps, few, HEAD_DIM)
    temporal = jnp.swapaxes(temporal, 0, 1).reshape(tokens, HEAD_DIM)

    land_logits = jnp.einsum("me,se->ms", q_land, k, preferred_element_type=F32) * SCALE
    own_top = jnp.max(land_logits, axis=-1, keepdims=True).astype(BF16)
    own_weights = jnp.exp(land_logits - own_top.astype(F32))
    own_total = jnp.sum(own_weights, axis=-1, keepdims=True)
    own_sum = jnp.dot(own_weights.astype(BF16), temporal, preferred_element_type=F32)
    high, low = halves(own_total)
    extra = jnp.pad(
        jnp.concatenate([own_top, high, low], axis=1), ((0, 0), (0, HEAD_DIM - 3))
    )
    own = jnp.concatenate([own_sum.astype(BF16), extra], axis=1)
    inverse = inverse_parts(q_land, k_land)
    parts = swap(own.reshape(plane, block, 2 * HEAD_DIM), PLANE)
    parts, inverse, k_late = lax.optimization_barrier((parts, inverse, k_land))
    summary = swap(combine(parts), PLANE)
    attend = token_weights(got, k_late)
    high, low = last_iteration(inverse)
    out = finish(high, low, summary, attend, temporal, steps, part)
    back = swap(out, ACROSS)
    return unpack(back, sides)[None]


def solution(mesh):
    tm, space = mesh.devices.shape
    fine = jax.sharding.Mesh(mesh.devices.reshape(tm // 2, 2, space), ("z", "core", "space"))
    block = P(("z", "core"), "space", None)
    return jax.shard_map(
        local,
        mesh=fine,
        in_specs=(block, block, block, P(("z", "core"), "space")),
        out_specs=block,
        check_vma=False,
    )
```

```python
import math

import jax
import jax.numpy as jnp
from jax import lax
from jax.experimental import pallas as pl
from jax.experimental.pallas import tpu as pltpu
from jax.sharding import PartitionSpec as P

HEAD_DIM = 128
LANDMARKS = 512
ITERS = 3
GROUP = 256
ACROSS = ("z", "core")
PLANE = ("core", "space")
SCALE = 1.0 / math.sqrt(HEAD_DIM)
F32 = jnp.float32
BF16 = jnp.bfloat16


def softmax_rows(logits):
    ceiling = jnp.max(logits, axis=-1, keepdims=True)
    expo = jnp.exp(logits - ceiling)
    return expo / jnp.sum(expo, axis=-1, keepdims=True)


def in_hbm(*arrays):
    return [pltpu.with_memory_space_constraint(x, pltpu.HBM) for x in arrays]


def halves(x):
    high = x.astype(BF16)
    return high, (x - high.astype(F32)).astype(BF16)


def triple(left, right):
    lh, ll = left
    rh, rl = right
    return jnp.dot(
        jnp.concatenate([lh, lh, ll], axis=1),
        jnp.concatenate([rh, rl, rh], axis=0),
        preferred_element_type=F32,
    )


def inverse_body(q_ref, k_ref, out_ref, kh_ref, kl_ref):
    dims = (((1,), (1,)), ((), ()))
    q, k = q_ref[...], k_ref[...]
    logits = lax.dot_general(q, k, dims, preferred_element_type=F32) * SCALE
    kernel = softmax_rows(logits)
    column_top = jnp.max(jnp.sum(kernel, axis=0, keepdims=True))
    kh_ref[...], kl_ref[...] = halves(kernel)
    logits = lax.dot_general(k, q, dims, preferred_element_type=F32) * SCALE
    expo = jnp.exp(logits - jnp.max(logits, axis=0, keepdims=True))
    out_ref[...] = expo / (jnp.sum(expo, axis=0, keepdims=True) * column_top)

    def step(_, carry):
        iterate = out_ref[...]
        z = halves(iterate)
        y = halves(triple((kh_ref[...], kl_ref[...]), z))
        first = triple(z, y)
        second = triple(halves(first), y)
        third = triple(halves(second), y)
        out_ref[...] = 0.25 * (13.0 * iterate - 15.0 * first + 7.0 * second - third)
        return carry

    lax.fori_loop(0, ITERS, step, 0)


def pseudo_inverse(q_land, k_land):
    whole = pl.BlockSpec(memory_space=pltpu.VMEM)
    return pl.pallas_call(
        inverse_body,
        out_shape=jax.ShapeDtypeStruct((LANDMARKS, LANDMARKS), F32),
        in_specs=[whole, whole],
        out_specs=whole,
        scratch_shapes=[pltpu.VMEM((LANDMARKS, LANDMARKS), BF16)] * 2,
        compiler_params=pltpu.CompilerParams(vmem_limit_bytes=32 * 2**20),
        cost_estimate=pl.CostEstimate(
            flops=12 * 3 * 2 * LANDMARKS**3, bytes_accessed=2 * 2**20, transcendentals=0
        ),
    )(q_land, k_land)


def pack_body(q_ref, k_ref, v_ref, id_ref, out_ref):
    sides, part = id_ref.shape
    quad = out_ref.shape[0] // sides
    row = lax.broadcasted_iota(jnp.int32, (16, part), 0)
    for side in range(sides):
        ids = id_ref[side : side + 1, :]
        coarse = lax.shift_right_logical(ids, 8)
        fine = ids - coarse * 256
        tile = jnp.where(row == 0, coarse, jnp.where(row == 1, fine, 0))
        tile = tile.astype(F32).astype(BF16)
        rows = slice(side * part, (side + 1) * part)
        for head in range(quad):
            lanes = slice(head * HEAD_DIM, (head + 1) * HEAD_DIM)
            chunk = head * sides + side
            out_ref[chunk, :part, :] = q_ref[rows, lanes]
            out_ref[chunk, part : 2 * part, :] = k_ref[rows, lanes]
            out_ref[chunk, 2 * part : 3 * part, :] = v_ref[rows, lanes]
            out_ref[chunk, 3 * part : 3 * part + 16, :] = tile


def pack(queries, keys, values, groups, sides):
    count, width = queries.shape
    part = count // sides
    quad = 4
    columns = quad * HEAD_DIM
    cut = pl.BlockSpec((count, columns), lambda i: (0, i))
    rows = 3 * part + 16
    chunks = width // HEAD_DIM * sides
    return pl.pallas_call(
        pack_body,
        grid=(width // columns,),
        out_shape=pltpu.HBM((chunks, rows, HEAD_DIM), BF16),
        in_specs=[cut, cut, cut, pl.BlockSpec((sides, part), lambda i: (0, 0))],
        out_specs=pl.BlockSpec((quad * sides, rows, HEAD_DIM), lambda i: (i, 0, 0)),
        compiler_params=pltpu.CompilerParams(vmem_limit_bytes=24 * 2**20),
    )(*in_hbm(queries, keys, values, groups.reshape(sides, part)))


def unpack_body(in_ref, out_ref):
    chunks, part, _ = in_ref.shape
    sides = out_ref.shape[0] // part
    for chunk in range(chunks):
        head, side = chunk // sides, chunk % sides
        rows = slice(side * part, (side + 1) * part)
        out_ref[rows, head * HEAD_DIM : (head + 1) * HEAD_DIM] = in_ref[chunk]


def unpack(x, sides):
    chunks, part, _ = x.shape
    quad = 4
    return pl.pallas_call(
        unpack_body,
        grid=(chunks // sides // quad,),
        out_shape=jax.ShapeDtypeStruct((sides * part, chunks // sides * HEAD_DIM), BF16),
        in_specs=[pl.BlockSpec((quad * sides, part, HEAD_DIM), lambda i: (i, 0, 0))],
        out_specs=pl.BlockSpec((sides * part, quad * HEAD_DIM), lambda i: (0, i)),
        compiler_params=pltpu.CompilerParams(vmem_limit_bytes=24 * 2**20),
    )(x)


def whole_call(body, out_shape, operands, megabytes, scratch=(), flops=0):
    size = sum(x.size * x.dtype.itemsize for x in operands)
    return pl.pallas_call(
        body,
        out_shape=out_shape,
        scratch_shapes=list(scratch),
        compiler_params=pltpu.CompilerParams(vmem_limit_bytes=megabytes * 2**20),
        cost_estimate=pl.CostEstimate(flops=flops, bytes_accessed=size, transcendentals=0),
    )(*operands)


def sums_body(got_ref, out_ref, acc_ref):
    several = got_ref.shape[0]
    part = (got_ref.shape[1] - 16) // 3
    plane, pair, _ = out_ref.shape
    block = pair // 2
    turn = pl.program_id(0)

    @pl.when(turn == 0)
    def _():
        acc_ref[...] = jnp.zeros_like(acc_ref)

    rows = lax.broadcasted_iota(jnp.int32, (LANDMARKS, part), 0)
    onehot, rest = [], []
    for frame in range(several):
        ids = got_ref[frame, 3 * part : 3 * part + 16, :].astype(F32)
        member = (ids[0:1, :] * 256.0 + ids[1:2, :]).astype(jnp.int32)
        onehot.append((rows == member).astype(F32).astype(BF16))
        rest.append(
            jnp.concatenate([got_ref[frame, :part, :], got_ref[frame, part : 2 * part, :]], axis=1)
        )
    acc_ref[...] += jnp.dot(
        jnp.concatenate(onehot, axis=1),
        jnp.concatenate(rest, axis=0),
        preferred_element_type=F32,
    )

    @pl.when(turn == pl.num_programs(0) - 1)
    def _():
        for side in range(2):
            x = acc_ref[:, side * HEAD_DIM : (side + 1) * HEAD_DIM].astype(BF16)
            out_ref[:, side * block : (side + 1) * block, :] = x.reshape(plane, block, HEAD_DIM)


def group_sums(got, plane):
    steps, rows, _ = got.shape
    several = 4
    pair = 2 * LANDMARKS // plane
    return pl.pallas_call(
        sums_body,
        grid=(steps // several,),
        out_shape=pltpu.HBM((plane, pair, HEAD_DIM), BF16),
        in_specs=[pl.BlockSpec((several, rows, HEAD_DIM), lambda i: (i, 0, 0))],
        out_specs=pl.BlockSpec((plane, pair, HEAD_DIM), lambda i: (0, 0, 0)),
        scratch_shapes=[pltpu.VMEM((LANDMARKS, 2 * HEAD_DIM), F32)],
        compiler_params=pltpu.CompilerParams(vmem_limit_bytes=12 * 2**20),
    )(got)


def mean_body(parts_ref, out_ref):
    total = jnp.sum(parts_ref[...].astype(F32), axis=0, keepdims=True)
    mean = (total / GROUP).astype(BF16)
    out_ref[...] = jnp.broadcast_to(mean, out_ref.shape)


def group_means(parts):
    return whole_call(mean_body, pltpu.HBM(parts.shape, BF16), [parts], 8)


def combine_body(parts_ref, out_ref):
    x = parts_ref[...].astype(F32)
    tops = x[:, :, HEAD_DIM : HEAD_DIM + 1]
    totals = x[:, :, HEAD_DIM + 1 : HEAD_DIM + 2] + x[:, :, HEAD_DIM + 2 : HEAD_DIM + 3]
    factor = jnp.exp(tops - jnp.max(tops, axis=0, keepdims=True))
    weighted = jnp.sum(x[:, :, :HEAD_DIM] * factor, axis=0, keepdims=True)
    total = jnp.sum(totals * factor, axis=0, keepdims=True)
    out_ref[...] = jnp.broadcast_to((weighted / total).astype(BF16), out_ref.shape)


def combine(parts):
    plane, block, _ = parts.shape
    return whole_call(
        combine_body, pltpu.HBM((plane, block, HEAD_DIM), BF16), [parts], 8
    )


def swap(x, axes):
    return lax.all_to_all(x, axes, split_axis=0, concat_axis=0, tiled=True)


def local(queries, keys, values, groups):
    frames, count, width = queries.shape
    heads = width // HEAD_DIM
    sides = lax.axis_size("core")
    steps = heads * sides
    part = count // sides
    tokens = steps * part
    plane = lax.axis_size(PLANE)
    block = LANDMARKS // plane

    packed = pack(queries[0], keys[0], values[0], groups, sides)
    got = swap(packed, ACROSS)
    q = got[:, :part].reshape(tokens, HEAD_DIM)
    k = got[:, part : 2 * part].reshape(tokens, HEAD_DIM)
    v = got[:, 2 * part : 3 * part].reshape(tokens, HEAD_DIM)
    lands = swap(group_means(swap(group_sums(got, plane), PLANE)), PLANE)
    q_land = lands[:, :block].reshape(LANDMARKS, HEAD_DIM)
    k_land = lands[:, block:].reshape(LANDMARKS, HEAD_DIM)

    few = 8

    def split(x):
        x = x.reshape(steps, part // few, few, HEAD_DIM)
        return jnp.swapaxes(x, 0, 1).reshape(part // few, steps * few, HEAD_DIM)

    logits = jnp.einsum("sae,sbe->sab", split(q), split(k), preferred_element_type=F32) * SCALE
    index = jnp.arange(steps * few, dtype=jnp.int32) % few
    logits = jnp.where(index[:, None] == index[None, :], logits, -jnp.inf)
    weights = softmax_rows(logits).astype(BF16)
    temporal = jnp.einsum("sab,sbe->sae", weights, split(v), preferred_element_type=F32)
    temporal = temporal.astype(BF16).reshape(part // few, steps, few, HEAD_DIM)
    temporal = jnp.swapaxes(temporal, 0, 1).reshape(tokens, HEAD_DIM)

    land_logits = jnp.einsum("me,se->ms", q_land, k, preferred_element_type=F32) * SCALE
    own_top = jnp.max(land_logits, axis=-1, keepdims=True).astype(BF16)
    own_weights = jnp.exp(land_logits - own_top.astype(F32))
    own_total = jnp.sum(own_weights, axis=-1, keepdims=True)
    own_sum = jnp.dot(own_weights.astype(BF16), temporal, preferred_element_type=F32)
    high, low = halves(own_total)
    extra = jnp.pad(
        jnp.concatenate([own_top, high, low], axis=1), ((0, 0), (0, HEAD_DIM - 3))
    )
    own = jnp.concatenate([own_sum.astype(BF16), extra], axis=1)
    parts = swap(own.reshape(plane, block, 2 * HEAD_DIM), PLANE)
    summary = swap(combine(parts), PLANE).reshape(LANDMARKS, HEAD_DIM).astype(F32)

    inverse = pseudo_inverse(q_land, k_land)
    token_logits = jnp.einsum("se,me->sm", q, k_land, preferred_element_type=F32) * SCALE
    attend = lax.optimization_barrier(softmax_rows(token_logits).astype(BF16))
    mixed = jnp.dot(inverse, summary, precision=lax.Precision.HIGHEST).astype(BF16)
    global_part = jnp.dot(attend, mixed, preferred_element_type=F32)
    combined = (temporal.astype(F32) + global_part).astype(BF16)
    back = swap(combined.reshape(steps, part, HEAD_DIM), ACROSS)
    return unpack(back, sides)[None]


def solution(mesh):
    tm, space = mesh.devices.shape
    fine = jax.sharding.Mesh(mesh.devices.reshape(tm // 2, 2, space), ("z", "core", "space"))
    block = P(("z", "core"), "space", None)
    return jax.shard_map(
        local,
        mesh=fine,
        in_specs=(block, block, block, P(("z", "core"), "space")),
        out_specs=block,
        check_vma=False,
    )
```

```python
import math

import jax
import jax.numpy as jnp
from jax import lax
from jax.experimental import pallas as pl
from jax.experimental.pallas import tpu as pltpu
from jax.sharding import PartitionSpec as P

HEAD_DIM = 128
LANDMARKS = 512
ITERS = 3
GROUP = 256
EXTRA = 8
ACROSS = ("z", "core")
PLANE = ("core", "space")
SCALE = 1.0 / math.sqrt(HEAD_DIM)
F32 = jnp.float32
BF16 = jnp.bfloat16


def softmax_rows(logits):
    ceiling = jnp.max(logits, axis=-1, keepdims=True)
    expo = jnp.exp(logits - ceiling)
    return expo / jnp.sum(expo, axis=-1, keepdims=True)


def in_hbm(*arrays):
    return [pltpu.with_memory_space_constraint(x, pltpu.HBM) for x in arrays]


def halves(x):
    high = x.astype(BF16)
    return high, (x - high.astype(F32)).astype(BF16)


def triple(left, right):
    lh, ll = left
    rh, rl = right
    return jnp.dot(
        jnp.concatenate([lh, lh, ll], axis=1),
        jnp.concatenate([rh, rl, rh], axis=0),
        preferred_element_type=F32,
    )


def inverse_body(q_ref, k_ref, out_ref, kh_ref, kl_ref):
    dims = (((1,), (1,)), ((), ()))
    q, k = q_ref[...], k_ref[...]
    logits = lax.dot_general(q, k, dims, preferred_element_type=F32) * SCALE
    kernel = softmax_rows(logits)
    column_top = jnp.max(jnp.sum(kernel, axis=0, keepdims=True))
    kh_ref[...], kl_ref[...] = halves(kernel)
    logits = lax.dot_general(k, q, dims, preferred_element_type=F32) * SCALE
    expo = jnp.exp(logits - jnp.max(logits, axis=0, keepdims=True))
    out_ref[...] = expo / (jnp.sum(expo, axis=0, keepdims=True) * column_top)

    def step(_, carry):
        iterate = out_ref[...]
        z = halves(iterate)
        y = halves(triple((kh_ref[...], kl_ref[...]), z))
        first = triple(z, y)
        second = triple(halves(first), y)
        third = triple(halves(second), y)
        out_ref[...] = 0.25 * (13.0 * iterate - 15.0 * first + 7.0 * second - third)
        return carry

    lax.fori_loop(0, ITERS, step, 0)


def pseudo_inverse(q_land, k_land):
    whole = pl.BlockSpec(memory_space=pltpu.VMEM)
    return pl.pallas_call(
        inverse_body,
        out_shape=jax.ShapeDtypeStruct((LANDMARKS, LANDMARKS), F32),
        in_specs=[whole, whole],
        out_specs=whole,
        scratch_shapes=[pltpu.VMEM((LANDMARKS, LANDMARKS), BF16)] * 2,
        compiler_params=pltpu.CompilerParams(vmem_limit_bytes=32 * 2**20),
        cost_estimate=pl.CostEstimate(
            flops=12 * 3 * 2 * LANDMARKS**3, bytes_accessed=2 * 2**20, transcendentals=0
        ),
    )(q_land, k_land)


def pack_body(q_ref, k_ref, v_ref, id_ref, out_ref):
    sides, part = id_ref.shape
    quad = out_ref.shape[0] // sides
    row = lax.broadcasted_iota(jnp.int32, (EXTRA, part), 0)
    for side in range(sides):
        ids = id_ref[side : side + 1, :]
        coarse = lax.shift_right_logical(ids, 8)
        fine = ids - coarse * 256
        tile = jnp.where(row == 0, coarse, jnp.where(row == 1, fine, 0))
        tile = tile.astype(F32).astype(BF16)
        rows = slice(side * part, (side + 1) * part)
        for head in range(quad):
            lanes = slice(head * HEAD_DIM, (head + 1) * HEAD_DIM)
            chunk = head * sides + side
            out_ref[chunk, :part, :] = q_ref[rows, lanes]
            out_ref[chunk, part : 2 * part, :] = k_ref[rows, lanes]
            out_ref[chunk, 2 * part : 3 * part, :] = v_ref[rows, lanes]
            out_ref[chunk, 3 * part : 3 * part + EXTRA, :] = tile


def pack(queries, keys, values, groups, sides):
    count, width = queries.shape
    part = count // sides
    quad = 2
    columns = quad * HEAD_DIM
    cut = pl.BlockSpec((count, columns), lambda i: (0, i))
    rows = 3 * part + EXTRA
    chunks = width // HEAD_DIM * sides
    return pl.pallas_call(
        pack_body,
        grid=(width // columns,),
        out_shape=pltpu.HBM((chunks, rows, HEAD_DIM), BF16),
        in_specs=[cut, cut, cut, pl.BlockSpec((sides, part), lambda i: (0, 0))],
        out_specs=pl.BlockSpec((quad * sides, rows, HEAD_DIM), lambda i: (i, 0, 0)),
        compiler_params=pltpu.CompilerParams(vmem_limit_bytes=24 * 2**20),
    )(*in_hbm(queries, keys, values, groups.reshape(sides, part)))


def unpack_body(in_ref, out_ref):
    chunks, part, _ = in_ref.shape
    sides = out_ref.shape[0] // part
    for chunk in range(chunks):
        head, side = chunk // sides, chunk % sides
        rows = slice(side * part, (side + 1) * part)
        out_ref[rows, head * HEAD_DIM : (head + 1) * HEAD_DIM] = in_ref[chunk]


def unpack(x, sides):
    chunks, part, _ = x.shape
    quad = 2
    return pl.pallas_call(
        unpack_body,
        grid=(chunks // sides // quad,),
        out_shape=jax.ShapeDtypeStruct((sides * part, chunks // sides * HEAD_DIM), BF16),
        in_specs=[pl.BlockSpec((quad * sides, part, HEAD_DIM), lambda i: (i, 0, 0))],
        out_specs=pl.BlockSpec((sides * part, quad * HEAD_DIM), lambda i: (0, i)),
        compiler_params=pltpu.CompilerParams(vmem_limit_bytes=24 * 2**20),
    )(x)


def whole_call(body, out_shape, operands, megabytes, scratch=(), flops=0):
    size = sum(x.size * x.dtype.itemsize for x in operands)
    return pl.pallas_call(
        body,
        out_shape=out_shape,
        scratch_shapes=list(scratch),
        compiler_params=pltpu.CompilerParams(vmem_limit_bytes=megabytes * 2**20),
        cost_estimate=pl.CostEstimate(flops=flops, bytes_accessed=size, transcendentals=0),
    )(*operands)


def sums_body(got_ref, out_ref, acc_ref):
    several = got_ref.shape[0]
    part = (got_ref.shape[1] - EXTRA) // 3
    plane, pair, _ = out_ref.shape
    block = pair // 2
    turn = pl.program_id(0)

    @pl.when(turn == 0)
    def _():
        acc_ref[...] = jnp.zeros_like(acc_ref)

    rows = lax.broadcasted_iota(jnp.int32, (LANDMARKS, part), 0)
    onehot, rest = [], []
    for frame in range(several):
        ids = got_ref[frame, 3 * part : 3 * part + EXTRA, :].astype(F32)
        member = (ids[0:1, :] * 256.0 + ids[1:2, :]).astype(jnp.int32)
        onehot.append((rows == member).astype(F32).astype(BF16))
        rest.append(
            jnp.concatenate([got_ref[frame, :part, :], got_ref[frame, part : 2 * part, :]], axis=1)
        )
    acc_ref[...] += jnp.dot(
        jnp.concatenate(onehot, axis=1),
        jnp.concatenate(rest, axis=0),
        preferred_element_type=F32,
    )

    @pl.when(turn == pl.num_programs(0) - 1)
    def _():
        for side in range(2):
            x = acc_ref[:, side * HEAD_DIM : (side + 1) * HEAD_DIM].astype(BF16)
            out_ref[:, side * block : (side + 1) * block, :] = x.reshape(plane, block, HEAD_DIM)


def group_sums(got, plane):
    steps, rows, _ = got.shape
    several = 4
    pair = 2 * LANDMARKS // plane
    return pl.pallas_call(
        sums_body,
        grid=(steps // several,),
        out_shape=pltpu.HBM((plane, pair, HEAD_DIM), BF16),
        in_specs=[pl.BlockSpec((several, rows, HEAD_DIM), lambda i: (i, 0, 0))],
        out_specs=pl.BlockSpec((plane, pair, HEAD_DIM), lambda i: (0, 0, 0)),
        scratch_shapes=[pltpu.VMEM((LANDMARKS, 2 * HEAD_DIM), F32)],
        compiler_params=pltpu.CompilerParams(vmem_limit_bytes=12 * 2**20),
    )(got)


def mean_body(parts_ref, out_ref):
    total = jnp.sum(parts_ref[...].astype(F32), axis=0, keepdims=True)
    mean = (total / GROUP).astype(BF16)
    out_ref[...] = jnp.broadcast_to(mean, out_ref.shape)


def group_means(parts):
    return whole_call(mean_body, pltpu.HBM(parts.shape, BF16), [parts], 8)


def combine_body(parts_ref, out_ref):
    x = parts_ref[...].astype(F32)
    tops = x[:, :, HEAD_DIM : HEAD_DIM + 1]
    totals = x[:, :, HEAD_DIM + 1 : HEAD_DIM + 2] + x[:, :, HEAD_DIM + 2 : HEAD_DIM + 3]
    factor = jnp.exp(tops - jnp.max(tops, axis=0, keepdims=True))
    weighted = jnp.sum(x[:, :, :HEAD_DIM] * factor, axis=0, keepdims=True)
    total = jnp.sum(totals * factor, axis=0, keepdims=True)
    out_ref[...] = jnp.broadcast_to((weighted / total).astype(BF16), out_ref.shape)


def combine(parts):
    plane, block, _ = parts.shape
    return whole_call(
        combine_body, pltpu.HBM((plane, block, HEAD_DIM), BF16), [parts], 8
    )


def swap(x, axes):
    return lax.all_to_all(x, axes, split_axis=0, concat_axis=0, tiled=True)


def local(queries, keys, values, groups):
    frames, count, width = queries.shape
    heads = width // HEAD_DIM
    sides = lax.axis_size("core")
    steps = heads * sides
    part = count // sides
    tokens = steps * part
    plane = lax.axis_size(PLANE)
    block = LANDMARKS // plane

    packed = pack(queries[0], keys[0], values[0], groups, sides)
    got = swap(packed, ACROSS)
    q = got[:, :part].reshape(tokens, HEAD_DIM)
    k = got[:, part : 2 * part].reshape(tokens, HEAD_DIM)
    v = got[:, 2 * part : 3 * part].reshape(tokens, HEAD_DIM)
    lands = swap(group_means(swap(group_sums(got, plane), PLANE)), PLANE)
    q_land = lands[:, :block].reshape(LANDMARKS, HEAD_DIM)
    k_land = lands[:, block:].reshape(LANDMARKS, HEAD_DIM)

    few = 8

    def split(x):
        x = x.reshape(steps, part // few, few, HEAD_DIM)
        return jnp.swapaxes(x, 0, 1).reshape(part // few, steps * few, HEAD_DIM)

    logits = jnp.einsum("sae,sbe->sab", split(q), split(k), preferred_element_type=F32) * SCALE
    index = jnp.arange(steps * few, dtype=jnp.int32) % few
    logits = jnp.where(index[:, None] == index[None, :], logits, -jnp.inf)
    weights = softmax_rows(logits).astype(BF16)
    temporal = jnp.einsum("sab,sbe->sae", weights, split(v), preferred_element_type=F32)
    temporal = temporal.astype(BF16).reshape(part // few, steps, few, HEAD_DIM)
    temporal = jnp.swapaxes(temporal, 0, 1).reshape(tokens, HEAD_DIM)

    land_logits = jnp.einsum("me,se->ms", q_land, k, preferred_element_type=F32) * SCALE
    own_top = jnp.max(land_logits, axis=-1, keepdims=True).astype(BF16)
    own_weights = jnp.exp(land_logits - own_top.astype(F32))
    own_total = jnp.sum(own_weights, axis=-1, keepdims=True)
    own_sum = jnp.dot(own_weights.astype(BF16), temporal, preferred_element_type=F32)
    high, low = halves(own_total)
    extra = jnp.pad(
        jnp.concatenate([own_top, high, low], axis=1), ((0, 0), (0, HEAD_DIM - 3))
    )
    own = jnp.concatenate([own_sum.astype(BF16), extra], axis=1)
    parts = swap(own.reshape(plane, block, 2 * HEAD_DIM), PLANE)
    summary = swap(combine(parts), PLANE).reshape(LANDMARKS, HEAD_DIM).astype(F32)

    inverse = pseudo_inverse(q_land, k_land)
    token_logits = jnp.einsum("se,me->sm", q, k_land, preferred_element_type=F32) * SCALE
    attend = lax.optimization_barrier(softmax_rows(token_logits).astype(BF16))
    mixed = jnp.dot(inverse, summary, precision=lax.Precision.HIGHEST).astype(BF16)
    global_part = jnp.dot(attend, mixed, preferred_element_type=F32)
    combined = (temporal.astype(F32) + global_part).astype(BF16)
    back = swap(combined.reshape(steps, part, HEAD_DIM), ACROSS)
    return unpack(back, sides)[None]


def solution(mesh):
    tm, space = mesh.devices.shape
    fine = jax.sharding.Mesh(mesh.devices.reshape(tm // 2, 2, space), ("z", "core", "space"))
    block = P(("z", "core"), "space", None)
    return jax.shard_map(
        local,
        mesh=fine,
        in_specs=(block, block, block, P(("z", "core"), "space")),
        out_specs=block,
        check_vma=False,
    )
```
